512 devices in a mesh: segment: 2 (over core), lat: 16 (over y, x_hi), lon: 16 (over x_lo, z).
Axes of the slice: x: 4 (x_hi: 2, x_lo: 2; x = x_hi * 2 + x_lo), y: 8, z: 8, core: 2. Of those that a mesh axis runs over, the one named last changes fastest.
Arguments:
- saved_inputs: bfloat16 [2, 2, 96, 384, 512], P('segment', None, 'lat', 'lon'), may hold values from -6 to 6
- cotangent: bfloat16 [2, 2, 96, 384, 512], P('segment', None, 'lat', 'lon'), may hold values from -6 to 6
- pole_mask: int32 [96], replicated, may hold values from 0 to 1, as said below
- bias_index: int32 [144, 144], replicated, may hold values from 0 to 758
- table_shallow: float32 [759, 8], replicated, may hold values from -8 to 253
- table_deep: float32 [759, 8], replicated, may hold values from -8 to 253
- qkv_shallow: bfloat16 [512, 1536], P('lat', 'lon'), may hold values from -0.25 to 0.25
- proj_shallow: bfloat16 [512, 512], P('lat', 'lon'), may hold values from -0.25 to 0.25
- qkv_deep: bfloat16 [1024, 1536], P('lat', 'lon'), may hold values from -0.1875 to 0.1875
- proj_deep: bfloat16 [512, 1024], P('lat', 'lon'), may hold values from -0.25 to 0.25
- adapters: float32 [2, 98304], P('segment'), may hold values from -0.3 to 0.3
Outputs:
- passed_input_gradients: bfloat16 [2, 2, 96, 384, 512], P('segment', None, 'lat', 'lon')
- adapter_grads: float32 [2, 98304], P('segment')
The draws below stay inside these ranges and needn't reach their ends.
Inputs may be any that keep to these rules, and one draw needn't show every extreme that they name: `pole_mask`: zero exactly on the first and on the last few rows (1 to 3 at each pole), one on all others.
All inputs are finite; a program needn't handle non-finite values.
Results may differ from the reference program's by a relative error of at most 0.014.
Values may be sent and summed in bfloat16 or wider, within the bound.
No kernel may reach another device: no remote copies, remote signals or barrier semaphores. Data moves between devices by JAX's collectives and lax.ppermute only.
A program may use at most 128 MiB of HBM per device.

```python
import jax
import jax.numpy as jnp
from jax import lax

D_S = 512
D_D = 1024
HEADS = 8
HEAD = 64
LEV = 2
WLAT = 6
WLON = 12
RS = 32
RD = 24
QKV = 1536
INNER = 512
WT = 144
NB = 759
NLAT = 96
NLON = 384
ADAPTER_ENTRIES = 98304


def perturbed_input(key, shape, share):
    first_key, second_key, random_key_three = jax.random.split(key, 3)
    base = 2.0 * jnp.clip(jax.random.normal(first_key, shape, jnp.float32), -4.0, 4.0)
    lifted = 3.0 * jax.random.uniform(second_key, shape, jnp.float32)
    chosen = jax.random.randint(random_key_three, shape, 0, share) == 0
    return jnp.where(chosen, lifted, base)


def draw_table_shallow(key, part):
    key = jax.random.fold_in(key, 21)
    return perturbed_input(key, (NB, HEADS), 1000000)


def draw_table_deep(key, part):
    key = jax.random.fold_in(key, 22)
    return perturbed_input(key, (NB, HEADS), 1000000)


def draw_pole_mask(key, part):
    key = jax.random.fold_in(key, 11)
    pads = jax.random.randint(key, (2,), 1, 4)
    row_ids = jnp.arange(NLAT, dtype=jnp.int32)
    return ((row_ids >= pads[0]) & (row_ids < NLAT - pads[1])).astype(jnp.int32)


def with_ends(drawn, stream_key, least, top_value):
    index_at = [jax.random.randint(jax.random.fold_in(stream_key, axis), (), 0, length) for axis, length in enumerate(drawn.shape)]
    main_axis = drawn.shape.index(max(drawn.shape))
    neighbour = index_at[:main_axis] + [(index_at[main_axis] + 1) % drawn.shape[main_axis]] + index_at[main_axis + 1:]
    return drawn.at[tuple(index_at)].set(least).at[tuple(neighbour)].set(top_value)


def block_levels(own_key, dims, cuts, low, largest):
    factor_of, own = 1.0, jax.random.fold_in(own_key, 6)
    for dim, blocks in cuts:
        heights = jnp.exp(jax.random.uniform(jax.random.fold_in(own, dim), (blocks,), jnp.float32, low / len(cuts), largest / len(cuts)))
        factor_of = factor_of * jnp.repeat(heights, dims[dim] // blocks).reshape([-1 if axis == dim else 1 for axis in range(len(dims))])
    return factor_of


def noise(stream_key, dims, deviation, bound, cuts=(), kind=jnp.bfloat16):
    factor_of = block_levels(stream_key, dims, cuts, -0.22, 0.18) if cuts else 1.0
    drawn = jax.random.normal(stream_key, dims, jnp.float32) * deviation * factor_of
    return jnp.minimum(jnp.maximum(drawn, -bound), bound).astype(kind)


def setup_inputs(seed: int = 0) -> dict:
    keys = jax.random.split(jax.random.key(seed), 12)
    saved_inputs = noise(keys[0], (2, LEV, NLAT, NLON, D_S), 1.0, 6.0, ((0, 2), (2, 16), (3, 16)))
    cotangent = noise(keys[1], (2, LEV, NLAT, NLON, D_S), 1.0, 6.0, ((0, 2), (2, 16), (3, 16)))
    pole_mask = draw_pole_mask(jax.random.fold_in(keys[11], 71), 0)
    bias_index = with_ends(jax.random.randint(keys[3], (WT, WT), 0, NB), jax.random.fold_in(keys[3], 1), 0, NB - 1).astype(jnp.int32)
    table_shallow = draw_table_shallow(jax.random.fold_in(keys[11], 71), 0)
    table_deep = draw_table_deep(jax.random.fold_in(keys[11], 71), 0)
    qkv_shallow = noise(keys[6], (D_S, QKV), D_S ** -0.5, 0.25, ((0, 16), (1, 16)))
    proj_shallow = noise(keys[7], (INNER, D_S), INNER ** -0.5, 0.25, ((0, 16), (1, 16)))
    qkv_deep = noise(keys[8], (D_D, QKV), D_D ** -0.5, 0.1875, ((0, 16), (1, 16)))
    proj_deep = noise(keys[9], (INNER, D_D), INNER ** -0.5, 0.25, ((0, 16), (1, 16)))
    adapters = noise(keys[10], (2, ADAPTER_ENTRIES), 0.05, 0.3, ((0, 2),), jnp.float32)
    return dict(saved_inputs=saved_inputs, cotangent=cotangent, pole_mask=pole_mask, bias_index=bias_index, table_shallow=table_shallow, table_deep=table_deep, qkv_shallow=qkv_shallow, proj_shallow=proj_shallow, qkv_deep=qkv_deep, proj_deep=proj_deep, adapters=adapters)


epsilon = 1e-05
precise = lax.Precision.HIGHEST

def unpack(flat_vector, shapes):
    split_portions = []
    offset = 0
    for row_count, col_count in shapes:
        split_portions.append(flat_vector[offset:offset + row_count * col_count].reshape(row_count, col_count))
        offset += row_count * col_count
    return split_portions

def to_windows(token_grid):
    levels, row_count, col_count, features = token_grid.shape
    split_grid = token_grid.reshape(levels, row_count // WLAT, WLAT, col_count // WLON, WLON, features)
    return split_grid.transpose(1, 3, 0, 2, 4, 5).reshape(-1, levels * WLAT * WLON, features)

def from_windows(windows, levels, row_count, col_count):
    features = windows.shape[-1]
    split_grid = windows.reshape(row_count // WLAT, col_count // WLON, levels, WLAT, WLON, features)
    return split_grid.transpose(2, 0, 3, 1, 4, 5).reshape(levels, row_count, col_count, features)

def row_tokens(row_values, levels, col_count):
    spread = jnp.broadcast_to(row_values[None, :, None, None], (levels, row_values.shape[0], col_count, 1))
    return to_windows(spread)[:, :, 0]

def window_block(token_grid, w_qkv, w_proj, table, bias_index, adapter_list, key_ok, region):
    levels, row_count, col_count, features = token_grid.shape
    a_qkv, b_qkv, a_proj, b_proj = adapter_list
    head_count = table.shape[1]
    windows = to_windows(token_grid)
    window_count = windows.shape[0]
    tokens = windows.shape[1]
    value_entries = windows.astype(jnp.float32).reshape(window_count * tokens, features)
    centred = value_entries - lax.optimization_barrier(jnp.mean(value_entries, axis=-1, keepdims=True))
    normed = (centred * lax.rsqrt(lax.optimization_barrier(jnp.mean(centred * centred, axis=-1, keepdims=True)) + epsilon)).astype(jnp.bfloat16)
    low_rank = jnp.dot(jnp.dot(normed.astype(jnp.float32), a_qkv, precision=precise), b_qkv, precision=precise)
    projected = (jnp.dot(normed, w_qkv, preferred_element_type=jnp.float32) + low_rank).astype(jnp.bfloat16)
    projected = projected.reshape(window_count, tokens, 3, head_count, HEAD)
    scores = jnp.einsum('wqhd,wkhd->whqk', projected[:, :, 0], projected[:, :, 1], preferred_element_type=jnp.float32) * HEAD ** (-0.5)
    pos_bias = jnp.take(table, bias_index, axis=0).transpose(2, 0, 1)
    scores = scores + pos_bias[None]
    key_valid = row_tokens(key_ok, levels, col_count)
    key_region = row_tokens(region, levels, col_count)
    allowed = (key_valid[:, None, :] > 0) & (key_region[:, :, None] == key_region[:, None, :])
    scores = jnp.where(allowed[:, None], scores, -1000000000.0)
    row_max = lax.optimization_barrier(jnp.max(scores, axis=-1, keepdims=True))
    exp_scores = jnp.exp(scores - row_max)
    attention = (exp_scores / lax.optimization_barrier(jnp.sum(exp_scores, axis=-1, keepdims=True))).astype(jnp.bfloat16)
    mixed_out = jnp.einsum('whqk,wkhd->wqhd', attention, projected[:, :, 2], preferred_element_type=jnp.float32)
    mixed_out = mixed_out.astype(jnp.bfloat16).reshape(window_count * tokens, head_count * HEAD)
    low_proj = jnp.dot(jnp.dot(mixed_out.astype(jnp.float32), a_proj, precision=precise), b_proj, precision=precise)
    result = value_entries + jnp.dot(mixed_out, w_proj, preferred_element_type=jnp.float32) + low_proj
    return from_windows(result.astype(jnp.bfloat16).reshape(window_count, tokens, features), levels, row_count, col_count)

def shift_masks(pole_mask):
    row_count = pole_mask.shape[0]
    row_ids = jnp.arange(row_count, dtype=jnp.int32)
    region = (row_ids + WLAT // 2 >= row_count).astype(jnp.int32)
    return (jnp.roll(pole_mask, -(WLAT // 2)), region)

def shallow_section(token_grid, flat_vector, w_qkv, w_proj, table, bias_index, pole_mask):
    shapes = ((D_S, RS), (RS, QKV), (INNER, RS), (RS, D_S))
    key_ok, region = shift_masks(pole_mask)
    rolled = jnp.roll(token_grid, (-(WLAT // 2), -(WLON // 2)), axis=(1, 2))
    out_grid = window_block(rolled, w_qkv, w_proj, table, bias_index, unpack(flat_vector, shapes), key_ok, region)
    return jnp.roll(out_grid, (WLAT // 2, WLON // 2), axis=(1, 2))

def deep_section(token_grid, flat_vector, w_qkv, w_proj, table, bias_index, pole_mask):
    shapes = ((D_D, RD), (RD, QKV), (INNER, RD), (RD, D_D))
    levels, row_count, col_count, features = token_grid.shape
    paired = token_grid.reshape(levels, row_count, col_count // 2, 2 * features)
    key_ok, region = shift_masks(pole_mask)
    rolled = jnp.roll(paired, (-(WLAT // 2), -(WLON // 2)), axis=(1, 2))
    out_grid = window_block(rolled, w_qkv, w_proj, table, bias_index, unpack(flat_vector, shapes), key_ok, region)
    out_grid = jnp.roll(out_grid, (WLAT // 2, WLON // 2), axis=(1, 2))
    return out_grid.reshape(levels, row_count, col_count, features)

def reference(saved_inputs, cotangent, pole_mask, bias_index, table_shallow, table_deep, qkv_shallow, proj_shallow, qkv_deep, proj_deep, adapters):

    def shallow_fn(token_grid, flat_vector):
        return shallow_section(token_grid, flat_vector, qkv_shallow, proj_shallow, table_shallow, bias_index, pole_mask)

    def deep_fn(token_grid, flat_vector):
        return deep_section(token_grid, flat_vector, qkv_deep, proj_deep, table_deep, bias_index, pole_mask)
    shallow_out, shallow_pull = jax.vjp(shallow_fn, saved_inputs[0], adapters[0])
    shallow_grad, shallow_adapt = shallow_pull(cotangent[0])
    deep_out, deep_pull = jax.vjp(deep_fn, saved_inputs[1], adapters[1])
    deep_grad, deep_adapt = deep_pull(cotangent[1])
    passed_input_gradients = jnp.stack([deep_grad, shallow_grad])
    adapter_grads = jnp.stack([shallow_adapt, deep_adapt])
    return (passed_input_gradients, adapter_grads)
```

```python
import functools

import jax
import jax.numpy as jnp
from jax import lax
from jax.experimental import pallas as pl
from jax.experimental.pallas import tpu as pltpu
from jax.sharding import PartitionSpec as P

WT = 144
HEADS = 8
HEAD = 64
QKV = 1536
INNER = 512
EPSILON = 1e-05
BF = jnp.bfloat16
F32 = jnp.float32
BOTH = ("lat", "lon")

PLACES = [(y, h, w, z) for y in range(8) for h in range(2) for w in range(2) for z in range(8)]
NUMBER = {place: i for i, place in enumerate(PLACES)}


def class_groups():
    groups = []
    for c in range(8):
        members = []
        for w in range(2):
            for z in range(8):
                for h in range(2):
                    members.append(NUMBER[((c - 4 * h - 2 * w - 3 * z) % 8, h, w, z)])
        groups.append(members)
    return groups


def neighbour_send(value, dx, dy, dz):
    route = []
    for y, h, w, z in PLACES:
        x = (2 * h + w + dx) % 4
        route.append((NUMBER[(y, h, w, z)], NUMBER[((y + dy) % 8, x // 2, x % 2, (z + dz) % 8)]))
    return lax.ppermute(value, BOTH, route)


def nt(a, b):
    return lax.dot_general(a, b, (((1,), (1,)), ((), ())), preferred_element_type=F32)


def nn(a, b):
    return lax.dot_general(a, b, (((1,), (0,)), ((), ())), preferred_element_type=F32)


def tn(a, b):
    return lax.dot_general(a, b, (((0,), (0,)), ((), ())), preferred_element_type=F32)


def window_row(shape, dim):
    token = lax.broadcasted_iota(jnp.int32, shape, dim)
    token = jnp.where(token >= 72, token - 72, token)
    row = jnp.zeros(shape, jnp.int32)
    for edge in range(12, 72, 12):
        row = row + (token >= edge).astype(jnp.int32)
    return row


def bias_kernel(place_ref, pole_ref, index_ref, table_ref, bias_ref, allowed_ref):
    for half in range(2):
        lanes = slice(128 * half, 128 * half + 128)
        index = index_ref[:, lanes]
        low = index & 127
        high = index >> 7
        for head in range(HEADS):
            found = jnp.zeros((WT, 128), F32)
            for chunk in range(6):
                entries = jnp.broadcast_to(
                    table_ref[head : head + 1, 128 * chunk : 128 * chunk + 128], (WT, 128)
                )
                taken = jnp.take_along_axis(entries, low, axis=1)
                found = taken if chunk == 0 else jnp.where(high == chunk, taken, found)
            bias_ref[head, :, lanes] = found
    first = place_ref[0] * 6 + 3
    key_row = window_row((WT, 256), 0)
    query_row = window_row((WT, 256), 1)
    key_ok = jnp.zeros((WT, 256), jnp.int32)
    key_region = jnp.zeros((WT, 256), jnp.int32)
    query_region = jnp.zeros((WT, 256), jnp.int32)
    for row in range(6):
        at = first + row
        moved = jnp.where(at >= 96, 1, 0)
        key_ok = jnp.where(key_row == row, pole_ref[at - 96 * moved], key_ok)
        key_region = jnp.where(key_row == row, moved, key_region)
        query_region = jnp.where(query_row == row, moved, query_region)
    good = (key_ok > 0) & (key_region == query_region)
    allowed_ref[...] = jnp.where(good, 1.0, 0.0)


def compact(wide):
    lane = lax.broadcasted_iota(jnp.int32, (wide.shape[0], 128), 1)
    chunks = []
    for group in range(4):
        a = [wide[:, 128 * (4 * group + i) : 128 * (4 * group + i) + 128] for i in range(4)]
        one = pltpu.roll(a[1], 96, 1)
        two = pltpu.roll(a[2], 64, 1)
        three = pltpu.roll(a[3], 32, 1)
        chunks.append(jnp.where(lane < 96, a[0], one))
        chunks.append(jnp.where(lane < 64, one, two))
        chunks.append(jnp.where(lane < 32, two, three))
    return chunks


def expand(chunks):
    lane = lax.broadcasted_iota(jnp.int32, chunks[0].shape, 1)
    wide = []
    for group in range(4):
        b = chunks[3 * group : 3 * group + 3]
        wide.append(jnp.where(lane < 96, b[0], 0.0))
        one = jnp.where(lane < 32, pltpu.roll(b[0], 32, 1), pltpu.roll(b[1], 32, 1))
        wide.append(jnp.where(lane < 96, one, 0.0))
        two = jnp.where(lane < 64, pltpu.roll(b[1], 64, 1), pltpu.roll(b[2], 64, 1))
        wide.append(jnp.where(lane < 96, two, 0.0))
        wide.append(jnp.where(lane < 96, pltpu.roll(b[2], 96, 1), 0.0))
    return [part.astype(BF) for part in wide]


def selector(shape, rank, k):
    row = lax.broadcasted_iota(jnp.int32, shape, 0)
    col = lax.broadcasted_iota(jnp.int32, shape, 1)
    if shape[0] == 32:
        hit = (row < rank) & (col == row + rank * k)
    else:
        hit = (col < rank) & (row == col + rank * k)
    return jnp.where(hit, 1.0, 0.0).astype(BF)


def block_kernel(
    deep,
    place_ref, p0, p1, p2, p3, p4a, p4b, p5, p6, p7,
    x_ref, c_ref, s1_ref, s2_ref, bias_ref, allowed_ref, adapter_ref,
    own_ref, side_ref, below_ref, corner_ref, grads_ref,
    weight, weight_p, xs, cs, cols, aq_s, ap_s, bq_s, bp_s, flat,
):
    features = 1024 if deep else 512
    rank = 24 if deep else 32
    windows = 1 if deep else 2
    tokens = WT * windows
    block = features // 16
    lanes_a = 384 if deep else 128
    strides = lanes_a // rank

    label = place_ref[1]
    for o, piece in enumerate((p0, p1, p2, p3, (p4a, p4b), p5, p6, p7)):
        for j in range(16):
            for h in range(2):
                y = lax.rem(label + o - 4 * h - 2 * (j // 8) - 3 * (j % 8) + 64, 8)
                at = pl.multiple_of((2 * y + h) * block, block)
                k = 2 * j + h
                if o == 4:
                    source = piece[0][k, :block] if k < 16 else piece[1][k - 16, :block]
                else:
                    source = piece[k, :block]
                weight[pl.ds(at, block), 128 * j : 128 * j + 128] = source
    quarter = lax.broadcasted_iota(jnp.int32, (block, 128), 1) // 32
    for j in range(16):
        for m in range(4):
            tile = jnp.zeros((block, 128), F32)
            for k in range(4):
                at = (4 * m + k) * block
                part = weight[at : at + block, 128 * j : 128 * j + 128].astype(F32)
                if k < 3:
                    part = pltpu.roll(part, 32 * (k + 1), 1)
                tile = jnp.where(quarter == k, part, tile)
            weight_p[block * j : block * j + block, 128 * m : 128 * m + 128] = tile.astype(BF)

    n_aq, n_bq = features * rank // 128, rank * 12
    n_ap, n_bp = 512 * rank // 128, rank * features // 128
    off_bq, off_ap, off_bp = n_aq, n_aq + n_bq, n_aq + n_bq + n_ap
    per = lanes_a // 128
    for off, rows, dest in ((0, n_aq, aq_s), (off_ap, n_ap, ap_s)):
        parts = [adapter_ref[pl.ds(off + c, rows // per, stride=per), :] for c in range(per)]
        packed = jnp.concatenate(parts, 1) if per > 1 else parts[0]
        packed = packed.astype(BF)
        for k in range(strides):
            dest[pl.ds(k, rows // per, stride=strides), :] = nn(packed, selector((lanes_a, 128), rank, k))
    if rank < 32:
        bq_s[...] = jnp.zeros_like(bq_s)
        bp_s[...] = jnp.zeros_like(bp_s)
    for c in range(12):
        bq_s[0:rank, 128 * c : 128 * c + 128] = adapter_ref[pl.ds(off_bq + c, rank, stride=12), :]
    for c in range(features // 128):
        bp_s[0:rank, 128 * c : 128 * c + 128] = adapter_ref[
            pl.ds(off_bp + c, rank, stride=features // 128), :
        ]
    a_qkv, b_qkv = aq_s[:, 0:32].astype(BF), bq_s[...].astype(BF)
    a_proj, b_proj = ap_s[:, 0:32].astype(BF), bp_s[...].astype(BF)

    for source, which, dest in ((x_ref, 0, xs), (c_ref, 1, cs)):
        for level in range(2):
            for row in range(6):
                if row < 3:
                    own = source[level, row + 3].astype(F32)
                else:
                    own = s1_ref[which, level, row - 3].astype(F32)
                side = s2_ref[which, level, row].astype(F32)
                at = 72 * level + 12 * row
                if deep:
                    for c in range(4):
                        lanes = slice(128 * c, 128 * c + 128)
                        cols[c, 0:12] = own[12:24, lanes]
                        cols[c, 12:24] = side[:, lanes]
                        for odd in range(2):
                            to = 512 * odd + 128 * c
                            dest[at : at + 12, to : to + 128] = cols[c, pl.ds(odd, 12, stride=2), :]
                else:
                    dest[at : at + 12, :] = own[6:18]
                    dest[at + 144 : at + 150, :] = own[18:24]
                    dest[at + 150 : at + 156, :] = side[0:6]

    x = xs[...]
    cot = cs[...]
    cot_b = cot.astype(BF)
    centred = x - jnp.mean(x, axis=1, keepdims=True)
    scale = lax.rsqrt(jnp.mean(centred * centred, axis=1, keepdims=True) + EPSILON)
    xhat = centred * scale
    normed = xhat.astype(BF)
    low_q = nn(normed, a_qkv).astype(BF)
    chunks = compact(nn(normed, weight[...]))
    low = nn(low_q, b_qkv)
    chunks = [chunks[c] + low[:, 128 * c : 128 * c + 128] for c in range(12)]
    low_c = nt(cot_b, b_proj).astype(BF)
    d_mixed = nn(cot_b, weight_p[...]) + nt(low_c, a_proj)

    lane = lax.broadcasted_iota(jnp.int32, (WT, 128), 1)
    allowed = allowed_ref[:, :WT] > 0.0
    mixed = [[None] * windows for _ in range(4)]
    d_chunks = [[None] * windows for _ in range(12)]
    for w in range(windows):
        rows = slice(WT * w, WT * w + WT)
        for pair in range(4):
            q = chunks[pair][rows].astype(BF)
            k = chunks[4 + pair][rows].astype(BF)
            v = chunks[8 + pair][rows].astype(BF)
            d_o = d_mixed[rows, 128 * pair : 128 * pair + 128].astype(BF)
            found = []
            for half in range(2):
                mine = (lane >= 64) if half else (lane < 64)
                q_half = jnp.where(mine, q * 0.125, jnp.zeros_like(q))
                v_half = jnp.where(mine, v, jnp.zeros_like(v))
                s = nt(k, q_half) + bias_ref[2 * pair + half, :, :WT]
                s = jnp.where(allowed, s, -1000000000.0)
                e = jnp.exp(s - jnp.max(s, axis=0, keepdims=True))
                p = e / jnp.sum(e, axis=0, keepdims=True)
                p_b = p.astype(BF)
                d_p = nt(v_half, d_o)
                d_s = p * (d_p - jnp.sum(d_p * p, axis=0, keepdims=True))
                d_s = jnp.where(allowed, d_s, 0.0).astype(BF)
                found.append((tn(p_b, v), tn(d_s, k), nn(d_s, q), nn(p_b, d_o)))
            both = [jnp.where(lane < 64, one, two) for one, two in zip(*found)]
            mixed[pair][w] = both[0].astype(BF)
            d_chunks[pair][w] = both[1] * 0.125
            d_chunks[4 + pair][w] = both[2] * 0.125
            d_chunks[8 + pair][w] = both[3]

    def joined(parts, axis):
        return parts[0] if len(parts) == 1 else jnp.concatenate(parts, axis)

    mixed = joined([joined(parts, 0) for parts in mixed], 1)
    d_chunks = [joined(parts, 0) for parts in d_chunks]
    d_proj = joined([part.astype(BF) for part in d_chunks], 1)

    low_m = nn(mixed, a_proj).astype(BF)
    back = nt(d_proj, b_qkv).astype(BF)
    d_wide = joined(expand(d_chunks), 1)
    d_n = nt(d_wide, weight[...]) + nt(back, a_qkv)
    mean_1 = jnp.mean(d_n, axis=1, keepdims=True)
    mean_2 = jnp.mean(d_n * xhat, axis=1, keepdims=True)
    xs[...] = cot + scale * (d_n - mean_1 - xhat * mean_2)

    aq_s[:, 0:32] = tn(normed, back)
    ap_s[:, 0:32] = tn(mixed, low_c)
    d_bq = tn(low_q, d_proj)
    d_bp = tn(low_m, cot_b)
    for off, rows, source in ((0, n_aq, aq_s), (off_ap, n_ap, ap_s)):
        total = jnp.zeros((rows // per, lanes_a), F32)
        for k in range(strides):
            part = source[pl.ds(k, rows // per, stride=strides), :][:, 0:32].astype(BF)
            total = total + nn(part, selector((32, lanes_a), rank, k))
        for c in range(per):
            flat[pl.ds(off + c, rows // per, stride=per), :] = total[:, 128 * c : 128 * c + 128]
    for c in range(12):
        flat[pl.ds(off_bq + c, rank, stride=12), :] = d_bq[0:rank, 128 * c : 128 * c + 128]
    for c in range(features // 128):
        flat[pl.ds(off_bp + c, rank, stride=features // 128), :] = d_bp[
            0:rank, 128 * c : 128 * c + 128
        ]
    grads_ref[...] = flat[...].astype(BF)

    for level in range(2):
        for row in range(6):
            at = 72 * level + 12 * row
            main, strip = (own_ref, side_ref) if row < 3 else (below_ref, corner_ref)
            if deep:
                for c in range(4):
                    lanes = slice(128 * c, 128 * c + 128)
                    for odd in range(2):
                        to = 512 * odd + 128 * c
                        cols[c, pl.ds(odd, 12, stride=2), :] = xs[at : at + 12, to : to + 128]
                    main[level, row % 3, 12:24, lanes] = cols[c, 0:12].astype(BF)
                    strip[level, row % 3, :, lanes] = cols[c, 12:24].astype(BF)
            else:
                for c in range(4):
                    lanes = slice(128 * c, 128 * c + 128)
                    cols[c, 0:6] = xs[at + 150 : at + 156, lanes]
                    cols[c, 6:18] = xs[at : at + 12, lanes]
                    cols[c, 18:24] = xs[at + 144 : at + 150, lanes]
                    whole = cols[c].astype(BF)
                    main[level, row % 3, :, lanes] = whole
                    strip[level, row % 3, :, lanes] = whole[0:12]


def run_block(deep, operands):
    features = 1024 if deep else 512
    tokens = WT if deep else 2 * WT
    spec = pl.BlockSpec(memory_space=pltpu.VMEM)
    return pl.pallas_call(
        functools.partial(block_kernel, deep),
        out_shape=(
            jax.ShapeDtypeStruct((2, 3, 24, 512), BF),
            jax.ShapeDtypeStruct((2, 3, 12, 512), BF),
            jax.ShapeDtypeStruct((2, 3, 24, 512), BF),
            jax.ShapeDtypeStruct((2, 3, 12, 512), BF),
            jax.ShapeDtypeStruct((768, 128), BF),
        ),
        in_specs=[pl.BlockSpec(memory_space=pltpu.SMEM)] + [spec] * (len(operands) - 1),
        out_specs=(spec,) * 5,
        scratch_shapes=[
            pltpu.VMEM((features, 2048), BF),
            pltpu.VMEM((features, 512), BF),
            pltpu.VMEM((tokens, features), F32),
            pltpu.VMEM((tokens, features), F32),
            pltpu.VMEM((4, 24, 128), F32),
            pltpu.VMEM((features, 128), F32),
            pltpu.VMEM((512, 128), F32),
            pltpu.VMEM((32, QKV), F32),
            pltpu.VMEM((32, features), F32),
            pltpu.VMEM((768, 128), F32),
        ],
        compiler_params=pltpu.CompilerParams(vmem_limit_bytes=56 * 1024 * 1024),
        name="deep_block" if deep else "shallow_block",
    )(*operands)


def sum_kernel(parts_ref, out_ref):
    total = parts_ref[0].astype(F32)
    for i in range(1, 16):
        total = total + parts_ref[i].astype(F32)
    out_ref[...] = jnp.broadcast_to(total.astype(BF)[None], out_ref.shape)


def summed(parts):
    return pl.pallas_call(
        sum_kernel,
        out_shape=jax.ShapeDtypeStruct((16, 48, 128), BF),
        in_specs=[pl.BlockSpec(memory_space=pltpu.VMEM)],
        out_specs=pl.BlockSpec(memory_space=pltpu.VMEM),
        name="sum_parts",
    )(parts)


def shards(
    saved_inputs, cotangent, pole_mask, bias_index, table_shallow, table_deep,
    qkv_shallow, proj_shallow, qkv_deep, proj_deep, adapters,
):
    segment = lax.axis_index("segment")
    lat = lax.axis_index("lat")
    lon = lax.axis_index("lon")
    x, cot = saved_inputs[0], cotangent[0]

    with jax.named_scope("pack"):
        shallow_w = jnp.concatenate([qkv_shallow, proj_shallow.T], 1)
        deep_w = jnp.concatenate([qkv_deep, proj_deep.T], 1)
        own_w = jnp.where(segment == 1, deep_w, jnp.pad(shallow_w, ((0, 32), (0, 0))))
        own_w = jnp.broadcast_to(own_w[None], (32, 64, 128))
    with jax.named_scope("halo_rows"):
        top = jnp.stack([x[:, :3], cot[:, :3]])
        s1 = lax.ppermute(top, "lat", [((i + 1) % 16, i) for i in range(16)])
    with jax.named_scope("weights_class"):
        piece = lax.all_to_all(own_w, BOTH, 0, 0, axis_index_groups=class_groups())
    with jax.named_scope("halo_columns"):
        left = jnp.stack([x[:, 3:, :12], cot[:, 3:, :12]])
        left = jnp.concatenate([left, s1[:, :, :, :12]], 2)
        s2 = lax.ppermute(left, "lon", [((i + 1) % 16, i) for i in range(16)])
    with jax.named_scope("weights_neighbours"):
        p6 = neighbour_send(piece, 1, 0, 0)
        p2 = neighbour_send(piece, -1, 0, 0)
        p7 = neighbour_send(piece, 0, 1, 0)
        p1 = neighbour_send(piece, 0, -1, 0)
        p5 = neighbour_send(piece, 0, 0, 1)
        p3 = neighbour_send(piece, 0, 0, -1)
        p4a = neighbour_send(piece[:16], 0, 1, 1)
        p4b = neighbour_send(piece[16:], 0, -1, -1)

    with jax.named_scope("bias"):
        label = (4 * (lat % 2) + 2 * (lon // 8) + lat // 2 + 3 * (lon % 8)) % 8
        place = jnp.stack([lat, label]).astype(jnp.int32)
        table = jnp.where(segment == 1, table_deep, table_shallow)
        table = jnp.pad(table.T, ((0, 0), (0, 768 - table.shape[0])))
        index = jnp.pad(bias_index.T, ((0, 0), (0, 256 - WT)))
        smem = pl.BlockSpec(memory_space=pltpu.SMEM)
        vmem = pl.BlockSpec(memory_space=pltpu.VMEM)
        bias, allowed = pl.pallas_call(
            bias_kernel,
            out_shape=(
                jax.ShapeDtypeStruct((HEADS, WT, 256), F32),
                jax.ShapeDtypeStruct((WT, 256), F32),
            ),
            in_specs=[smem, smem, vmem, vmem],
            out_specs=(vmem, vmem),
            name="bias_table",
        )(place, pole_mask, index, table)

    flat = adapters.reshape(768, 128)
    operands = (
        place, piece, p1, p2, p3, p4a, p4b, p5, p6, p7, x, cot, s1, s2, bias, allowed, flat,
    )
    own, side, below, corner, grads = lax.cond(
        segment == 0,
        functools.partial(run_block, False),
        functools.partial(run_block, True),
        operands,
    )

    every = ("segment", "lat", "lon")

    def hand(value, d_lat, d_lon):
        route = []
        for s in range(2):
            for a in range(16):
                for b in range(16):
                    to = (1 - s) * 256 + (a + d_lat) % 16 * 16 + (b + d_lon) % 16
                    route.append((s * 256 + a * 16 + b, to))
        return lax.ppermute(value, every, route)

    with jax.named_scope("hand_over"):
        own = hand(own, 0, 0)
        side = hand(side, 0, 1)
        below = hand(below, 1, 0)
        corner = hand(corner, 1, 1)
    with jax.named_scope("adapter_sum"):
        grads = lax.all_to_all(grads.reshape(16, 48, 128), "lon", 0, 0)
        grads = lax.all_to_all(summed(grads), "lat", 0, 0)
        grads = lax.all_to_all(summed(grads), "lon", 0, 0)
        adapter_sum = grads.astype(F32).reshape(1, 98304)
    with jax.named_scope("assemble"):
        edge = jnp.where(segment == 0, 12, 6)
        column = lax.broadcasted_iota(jnp.int32, (1, 1, 24, 1), 2)
        main = jnp.concatenate([below, own], 1)
        strip = jnp.concatenate([corner, side], 1)
        strip = jnp.pad(strip, ((0, 0), (0, 0), (0, 12), (0, 0)))
        gradient = jnp.where(column < edge, strip, main)
    return gradient[None], adapter_sum


def solution(mesh):
    tokens = P("segment", None, "lat", "lon", None)
    in_specs = (
        tokens, tokens, P(), P(), P(), P(),
        P("lat", "lon"), P("lat", "lon"), P("lat", "lon"), P("lat", "lon"), P("segment", None),
    )
    return jax.shard_map(
        shards, mesh=mesh, in_specs=in_specs, out_specs=(tokens, P("segment", None)), check_vma=False
    )
```

```python
import functools

import jax
import jax.numpy as jnp
from jax import lax
from jax.experimental import pallas as pl
from jax.experimental.pallas import tpu as pltpu
from jax.sharding import PartitionSpec as P

WT = 144
HEADS = 8
HEAD = 64
QKV = 1536
INNER = 512
EPSILON = 1e-05
BF = jnp.bfloat16
F32 = jnp.float32
BOTH = ("lat", "lon")

PLACES = [(y, h, w, z) for y in range(8) for h in range(2) for w in range(2) for z in range(8)]
NUMBER = {place: i for i, place in enumerate(PLACES)}


def class_groups():
    groups = []
    for c in range(8):
        members = []
        for w in range(2):
            for z in range(8):
                for h in range(2):
                    members.append(NUMBER[((c - 4 * h - 2 * w - 3 * z) % 8, h, w, z)])
        groups.append(members)
    return groups


def neighbour_send(value, dx, dy, dz):
    route = []
    for y, h, w, z in PLACES:
        x = (2 * h + w + dx) % 4
        route.append((NUMBER[(y, h, w, z)], NUMBER[((y + dy) % 8, x // 2, x % 2, (z + dz) % 8)]))
    return lax.ppermute(value, BOTH, route)


def nt(a, b):
    return lax.dot_general(a, b, (((1,), (1,)), ((), ())), preferred_element_type=F32)


def nn(a, b):
    return lax.dot_general(a, b, (((1,), (0,)), ((), ())), preferred_element_type=F32)


def tn(a, b):
    return lax.dot_general(a, b, (((0,), (0,)), ((), ())), preferred_element_type=F32)


def pack_kernel(place_ref, qs_ref, ps_ref, qd_ref, pd_ref, out_ref):
    @pl.when(place_ref[2] == 0)
    def _():
        out_ref[0, 0:32, 0:96] = qs_ref[...]
        out_ref[0, 0:32, 96:128] = ps_ref[...].astype(F32).T.astype(BF)
        out_ref[0, 32:64, :] = jnp.zeros((32, 128), BF)

    @pl.when(place_ref[2] == 1)
    def _():
        out_ref[0, :, 0:96] = qd_ref[...]
        out_ref[0, :, 96:128] = pd_ref[...].astype(F32).T.astype(BF)

    own = out_ref[0]
    for i in range(1, 32):
        out_ref[i] = own


def window_row(shape, dim):
    token = lax.broadcasted_iota(jnp.int32, shape, dim)
    token = jnp.where(token >= 72, token - 72, token)
    row = jnp.zeros(shape, jnp.int32)
    for edge in range(12, 72, 12):
        row = row + (token >= edge).astype(jnp.int32)
    return row


def bias_kernel(place_ref, pole_ref, index_ref, table_ref, bias_ref, allowed_ref):
    for half in range(2):
        lanes = slice(128 * half, 128 * half + 128)
        index = index_ref[:, lanes]
        low = index & 127
        high = index >> 7
        for head in range(HEADS):
            found = jnp.zeros((WT, 128), F32)
            for chunk in range(6):
                entries = jnp.broadcast_to(
                    table_ref[head : head + 1, 128 * chunk : 128 * chunk + 128], (WT, 128)
                )
                taken = jnp.take_along_axis(entries, low, axis=1)
                found = taken if chunk == 0 else jnp.where(high == chunk, taken, found)
            bias_ref[head, :, lanes] = found
    first = place_ref[0] * 6 + 3
    key_row = window_row((WT, 256), 0)
    query_row = window_row((WT, 256), 1)
    key_ok = jnp.zeros((WT, 256), jnp.int32)
    key_region = jnp.zeros((WT, 256), jnp.int32)
    query_region = jnp.zeros((WT, 256), jnp.int32)
    for row in range(6):
        at = first + row
        moved = jnp.where(at >= 96, 1, 0)
        key_ok = jnp.where(key_row == row, pole_ref[at - 96 * moved], key_ok)
        key_region = jnp.where(key_row == row, moved, key_region)
        query_region = jnp.where(query_row == row, moved, query_region)
    good = (key_ok > 0) & (key_region == query_region)
    allowed_ref[...] = jnp.where(good, 1.0, 0.0)


def compact(wide):
    lane = lax.broadcasted_iota(jnp.int32, (wide.shape[0], 128), 1)
    chunks = []
    for group in range(4):
        a = [wide[:, 128 * (4 * group + i) : 128 * (4 * group + i) + 128] for i in range(4)]
        one = pltpu.roll(a[1], 96, 1)
        two = pltpu.roll(a[2], 64, 1)
        three = pltpu.roll(a[3], 32, 1)
        chunks.append(jnp.where(lane < 96, a[0], one))
        chunks.append(jnp.where(lane < 64, one, two))
        chunks.append(jnp.where(lane < 32, two, three))
    return chunks


def expand(chunks):
    lane = lax.broadcasted_iota(jnp.int32, chunks[0].shape, 1)
    wide = []
    for group in range(4):
        b = chunks[3 * group : 3 * group + 3]
        wide.append(jnp.where(lane < 96, b[0], 0.0))
        one = jnp.where(lane < 32, pltpu.roll(b[0], 32, 1), pltpu.roll(b[1], 32, 1))
        wide.append(jnp.where(lane < 96, one, 0.0))
        two = jnp.where(lane < 64, pltpu.roll(b[1], 64, 1), pltpu.roll(b[2], 64, 1))
        wide.append(jnp.where(lane < 96, two, 0.0))
        wide.append(jnp.where(lane < 96, pltpu.roll(b[2], 96, 1), 0.0))
    return [part.astype(BF) for part in wide]


def selector(shape, rank, k):
    row = lax.broadcasted_iota(jnp.int32, shape, 0)
    col = lax.broadcasted_iota(jnp.int32, shape, 1)
    if shape[0] == 32:
        hit = (row < rank) & (col == row + rank * k)
    else:
        hit = (col < rank) & (row == col + rank * k)
    return jnp.where(hit, 1.0, 0.0).astype(BF)


def sizes(deep):
    features, rank, windows = (1024, 24, 1) if deep else (512, 32, 2)
    counts = (features * rank // 128, rank * 12, 512 * rank // 128, rank * features // 128)
    starts = (0, counts[0], sum(counts[:2]), sum(counts[:3]))
    return features, rank, windows, counts, starts


def by_half(deep, ref):
    return jnp.concatenate([ref[0:WT], ref[WT : 2 * WT]], 1) if deep else ref[...]


def prep_kernel(
    deep,
    x_ref, c_ref, s1_ref, s2_ref, s3_ref, adapter_ref,
    normed_ref, cot_ref, scale_ref, low_q_ref, low_c_ref, aq_ref, bq_ref, ap_ref,
    xs, cols, aq_s, ap_s, bq_s, bp_s,
):
    features, rank, windows, counts, starts = sizes(deep)
    wide_row = 384 if deep else 128
    steps, per = wide_row // rank, wide_row // 128

    for i, dest in ((0, aq_s), (2, ap_s)):
        n = counts[i] // per
        parts = [adapter_ref[pl.ds(starts[i] + c, n, stride=per), :] for c in range(per)]
        packed = jnp.concatenate(parts, 1) if per > 1 else parts[0]
        packed = packed.astype(BF)
        for k in range(steps):
            dest[pl.ds(k, n, stride=steps), :] = nn(packed, selector((wide_row, 128), rank, k))
    if rank < 32:
        bq_s[...] = jnp.zeros_like(bq_s)
        bp_s[...] = jnp.zeros_like(bp_s)
    for c in range(12):
        bq_s[0:rank, 128 * c : 128 * c + 128] = adapter_ref[
            pl.ds(starts[1] + c, rank, stride=12), :
        ]
    for c in range(features // 128):
        bp_s[0:rank, 128 * c : 128 * c + 128] = adapter_ref[
            pl.ds(starts[3] + c, rank, stride=features // 128), :
        ]
    a_qkv = aq_s[0:features, 0:32].astype(BF)
    aq_ref[0:features] = a_qkv
    bq_ref[...] = bq_s[...].astype(BF)
    ap_ref[...] = ap_s[:, 0:32].astype(BF)
    b_proj = bp_s[:, 0:features].astype(BF)

    for source, which in ((c_ref, 1), (x_ref, 0)):
        for level in range(2):
            for row in range(6):
                if row < 3:
                    own = source[level, row + 3].astype(F32)
                else:
                    own = s1_ref[which, level, row - 3].astype(F32)
                strip = s2_ref if row < 3 else s3_ref
                side = strip[which, level, row % 3].astype(F32)
                at = 72 * level + 12 * row
                if deep:
                    for c in range(4):
                        lanes = slice(128 * c, 128 * c + 128)
                        cols[c, 0:12] = own[12:24, lanes]
                        cols[c, 12:24] = side[:, lanes]
                        for odd in range(2):
                            to = WT * odd + at
                            xs[to : to + 12, lanes] = cols[c, pl.ds(odd, 12, stride=2), :]
                else:
                    xs[at : at + 12, :] = own[6:18]
                    xs[at + 144 : at + 150, :] = own[18:24]
                    xs[at + 150 : at + 156, :] = side[0:6]
        if which == 1:
            cot_ref[...] = xs[...].astype(BF)
    x = by_half(deep, xs)
    centred = x - jnp.mean(x, axis=1, keepdims=True)
    scale = lax.rsqrt(jnp.mean(centred * centred, axis=1, keepdims=True) + EPSILON)
    normed = (centred * scale).astype(BF)
    if deep:
        normed_ref[0:WT] = normed[:, 0:512]
        normed_ref[WT : 2 * WT] = normed[:, 512:1024]
    else:
        normed_ref[...] = normed
    tokens = WT * windows
    scale_ref[0:tokens] = jnp.broadcast_to(scale, (tokens, 128))
    low_q_ref[0:tokens] = nn(normed, a_qkv).astype(BF)
    low_c_ref[0:tokens] = nt(by_half(deep, cot_ref), b_proj).astype(BF)


def block_kernel(
    deep,
    place_ref, p0, p1, p2, p3, p4, p5, p6, p7, bias_ref, allowed_ref,
    normed_ref, cot_ref, scale_ref, low_q_ref, low_c_ref, aq_ref, bq_ref, ap_ref,
    own_ref, side_ref, below_ref, corner_ref, grads_ref,
    weight, weight_p, xs, cols, aq_s, ap_s, flat,
):
    features, rank, windows, counts, starts = sizes(deep)
    wide_row = 384 if deep else 128
    steps, per = wide_row // rank, wide_row // 128
    tokens = WT * windows
    block = features // 16

    label = place_ref[1]
    for o, piece in enumerate((p0, p1, p2, p3, p4, p5, p6, p7)):
        for j in range(16):
            for h in range(2):
                y = lax.rem(label + o - 4 * h - 2 * (j // 8) - 3 * (j % 8) + 64, 8)
                at = pl.multiple_of((2 * y + h) * block, block)
                weight[pl.ds(at, block), 128 * j : 128 * j + 128] = piece[2 * j + h, :block]
    quarter = lax.broadcasted_iota(jnp.int32, (block, 128), 1) // 32
    for j in range(16):
        for m in range(4):
            tile = jnp.zeros((block, 128), F32)
            for k in range(4):
                at = (4 * m + k) * block
                part = weight[at : at + block, 128 * j : 128 * j + 128].astype(F32)
                if k < 3:
                    part = pltpu.roll(part, 32 * (k + 1), 1)
                tile = jnp.where(quarter == k, part, tile)
            weight_p[block * j : block * j + block, 128 * m : 128 * m + 128] = tile.astype(BF)

    normed = by_half(deep, normed_ref)
    cot_b = by_half(deep, cot_ref)
    low_q, low_c = low_q_ref[0:tokens], low_c_ref[0:tokens]
    a_qkv, b_qkv, a_proj = aq_ref[0:features], bq_ref[...], ap_ref[...]
    chunks = compact(nn(normed, weight[...]))
    low = nn(low_q, b_qkv)
    chunks = [chunks[c] + low[:, 128 * c : 128 * c + 128] for c in range(12)]
    d_mixed = nn(cot_b, weight_p[...]) + nt(low_c, a_proj)

    lane = lax.broadcasted_iota(jnp.int32, (WT, 128), 1)
    allowed = allowed_ref[:, :WT] > 0.0
    mixed = [[None] * windows for _ in range(4)]
    d_chunks = [[None] * windows for _ in range(12)]
    for w in range(windows):
        rows = slice(WT * w, WT * w + WT)
        for pair in range(4):
            q = chunks[pair][rows].astype(BF)
            k = chunks[4 + pair][rows].astype(BF)
            v = chunks[8 + pair][rows].astype(BF)
            d_o = d_mixed[rows, 128 * pair : 128 * pair + 128].astype(BF)
            found = []
            for half in range(2):
                mine = (lane >= 64) if half else (lane < 64)
                q_half = jnp.where(mine, q * 0.125, jnp.zeros_like(q))
                v_half = jnp.where(mine, v, jnp.zeros_like(v))
                s = nt(k, q_half) + bias_ref[2 * pair + half, :, :WT]
                s = jnp.where(allowed, s, -1000000000.0)
                e = jnp.exp(s - jnp.max(s, axis=0, keepdims=True))
                p = e / jnp.sum(e, axis=0, keepdims=True)
                p_b = p.astype(BF)
                d_p = nt(v_half, d_o)
                d_s = p * (d_p - jnp.sum(d_p * p, axis=0, keepdims=True))
                d_s = jnp.where(allowed, d_s, 0.0).astype(BF)
                found.append((tn(p_b, v), tn(d_s, k), nn(d_s, q), nn(p_b, d_o)))
            both = [jnp.where(lane < 64, one, two) for one, two in zip(*found)]
            mixed[pair][w] = both[0].astype(BF)
            d_chunks[pair][w] = both[1] * 0.125
            d_chunks[4 + pair][w] = both[2] * 0.125
            d_chunks[8 + pair][w] = both[3]

    def joined(parts, axis):
        return parts[0] if len(parts) == 1 else jnp.concatenate(parts, axis)

    mixed = joined([joined(parts, 0) for parts in mixed], 1)
    d_chunks = [joined(parts, 0) for parts in d_chunks]
    d_proj = joined([part.astype(BF) for part in d_chunks], 1)

    low_m = nn(mixed, a_proj).astype(BF)
    back = nt(d_proj, b_qkv).astype(BF)
    d_wide = joined(expand(d_chunks), 1)
    d_n = nt(d_wide, weight[...]) + nt(back, a_qkv)
    xhat = normed.astype(F32)
    mean_1 = jnp.mean(d_n, axis=1, keepdims=True)
    mean_2 = jnp.mean(d_n * xhat, axis=1, keepdims=True)
    scale = scale_ref[0:tokens, 0:1]
    xs[...] = cot_b.astype(F32) + scale * (d_n - mean_1 - xhat * mean_2)

    aq_s[:, 0:32] = tn(normed, back)
    ap_s[:, 0:32] = tn(mixed, low_c)
    d_bq = tn(low_q, d_proj)
    d_bp = tn(low_m, cot_b)
    for i, source in ((0, aq_s), (2, ap_s)):
        n = counts[i] // per
        total = jnp.zeros((n, wide_row), F32)
        for k in range(steps):
            part = source[pl.ds(k, n, stride=steps), :][:, 0:32].astype(BF)
            total = total + nn(part, selector((32, wide_row), rank, k))
        for c in range(per):
            flat[pl.ds(starts[i] + c, n, stride=per), :] = total[:, 128 * c : 128 * c + 128]
    for c in range(12):
        flat[pl.ds(starts[1] + c, rank, stride=12), :] = d_bq[0:rank, 128 * c : 128 * c + 128]
    for c in range(features // 128):
        flat[pl.ds(starts[3] + c, rank, stride=features // 128), :] = d_bp[
            0:rank, 128 * c : 128 * c + 128
        ]
    grads_ref[...] = flat[...].astype(BF)

    for level in range(2):
        for row in range(6):
            at = 72 * level + 12 * row
            main, strip = (own_ref, side_ref) if row < 3 else (below_ref, corner_ref)
            if deep:
                for c in range(4):
                    lanes = slice(128 * c, 128 * c + 128)
                    for odd in range(2):
                        to = 512 * odd + 128 * c
                        cols[c, pl.ds(odd, 12, stride=2), :] = xs[at : at + 12, to : to + 128]
                    main[level, row % 3, 12:24, lanes] = cols[c, 0:12].astype(BF)
                    strip[level, row % 3, :, lanes] = cols[c, 12:24].astype(BF)
            else:
                for c in range(4):
                    lanes = slice(128 * c, 128 * c + 128)
                    cols[c, 0:6] = xs[at + 150 : at + 156, lanes]
                    cols[c, 6:18] = xs[at : at + 12, lanes]
                    cols[c, 18:24] = xs[at + 144 : at + 150, lanes]
                    whole = cols[c].astype(BF)
                    main[level, row % 3, :, lanes] = whole
                    strip[level, row % 3, :, lanes] = whole[0:12]


VMEM = pl.BlockSpec(memory_space=pltpu.VMEM)
SMEM = pl.BlockSpec(memory_space=pltpu.SMEM)


def run_prep(deep, operands):
    features = 1024 if deep else 512
    shapes = (
        ((2 * WT, 512), BF), ((2 * WT, 512), BF), ((2 * WT, 128), F32), ((2 * WT, 32), BF),
        ((2 * WT, 32), BF), ((1024, 32), BF), ((32, QKV), BF), ((512, 32), BF),
    )
    return pl.pallas_call(
        functools.partial(prep_kernel, deep),
        out_shape=tuple(jax.ShapeDtypeStruct(*shape) for shape in shapes),
        in_specs=[VMEM] * len(operands),
        out_specs=(VMEM,) * len(shapes),
        scratch_shapes=[
            pltpu.VMEM((2 * WT, 512), F32),
            pltpu.VMEM((4, 24, 128), F32),
            pltpu.VMEM((features, 128), F32),
            pltpu.VMEM((512, 128), F32),
            pltpu.VMEM((32, QKV), F32),
            pltpu.VMEM((32, features), F32),
        ],
        compiler_params=pltpu.CompilerParams(vmem_limit_bytes=32 * 1024 * 1024),
        name="deep_prep" if deep else "shallow_prep",
    )(*operands)


def run_block(deep, operands):
    features = 1024 if deep else 512
    tokens = WT if deep else 2 * WT
    shapes = (
        ((2, 3, 24, 512), BF), ((2, 3, 12, 512), BF), ((2, 3, 24, 512), BF),
        ((2, 3, 12, 512), BF), ((768, 128), BF),
    )
    return pl.pallas_call(
        functools.partial(block_kernel, deep),
        out_shape=tuple(jax.ShapeDtypeStruct(*shape) for shape in shapes),
        in_specs=[SMEM] + [VMEM] * (len(operands) - 1),
        out_specs=(VMEM,) * 5,
        scratch_shapes=[
            pltpu.VMEM((features, 2048), BF),
            pltpu.VMEM((features, 512), BF),
            pltpu.VMEM((tokens, features), F32),
            pltpu.VMEM((4, 24, 128), F32),
            pltpu.VMEM((features, 128), F32),
            pltpu.VMEM((512, 128), F32),
            pltpu.VMEM((768, 128), F32),
        ],
        compiler_params=pltpu.CompilerParams(vmem_limit_bytes=56 * 1024 * 1024),
        name="deep_block" if deep else "shallow_block",
    )(*operands)


def sum_kernel(parts_ref, out_ref):
    total = parts_ref[0].astype(F32)
    for i in range(1, 16):
        total = total + parts_ref[i].astype(F32)
    out_ref[...] = jnp.broadcast_to(total.astype(BF)[None], out_ref.shape)


def summed(parts):
    return pl.pallas_call(
        sum_kernel,
        out_shape=jax.ShapeDtypeStruct((16, 48, 128), BF),
        in_specs=[pl.BlockSpec(memory_space=pltpu.VMEM)],
        out_specs=pl.BlockSpec(memory_space=pltpu.VMEM),
        name="sum_parts",
    )(parts)


def hand(value, d_lat, d_lon):
    route = []
    for s in range(2):
        for a in range(16):
            for b in range(16):
                to = (1 - s) * 256 + (a + d_lat) % 16 * 16 + (b + d_lon) % 16
                route.append((s * 256 + a * 16 + b, to))
    return lax.ppermute(value, ("segment", "lat", "lon"), route)


def shift(value, d_lat, d_lon):
    route = []
    for a in range(16):
        for b in range(16):
            route.append((a * 16 + b, (a + d_lat) % 16 * 16 + (b + d_lon) % 16))
    return lax.ppermute(value, BOTH, route)


def shards(
    saved_inputs, cotangent, pole_mask, bias_index, table_shallow, table_deep,
    qkv_shallow, proj_shallow, qkv_deep, proj_deep, adapters,
):
    segment = lax.axis_index("segment")
    lat = lax.axis_index("lat")
    lon = lax.axis_index("lon")
    x, cot = saved_inputs[0], cotangent[0]

    label = (4 * (lat % 2) + 2 * (lon // 8) + lat // 2 + 3 * (lon % 8)) % 8
    place = jnp.stack([lat, label, segment]).astype(jnp.int32)
    with jax.named_scope("pack"):
        own_w = pl.pallas_call(
            pack_kernel,
            out_shape=jax.ShapeDtypeStruct((32, 64, 128), BF),
            in_specs=[SMEM] + [VMEM] * 4,
            out_specs=VMEM,
            name="pack_weights",
        )(place, qkv_shallow, proj_shallow, qkv_deep, proj_deep)
    with jax.named_scope("weights_class"):
        piece = lax.all_to_all(own_w, BOTH, 0, 0, axis_index_groups=class_groups())
    with jax.named_scope("halos"):
        s1 = shift(jnp.stack([x[:, :3], cot[:, :3]]), -1, 0)
        s2 = shift(jnp.stack([x[:, 3:, :12], cot[:, 3:, :12]]), 0, -1)
        s3 = shift(jnp.stack([x[:, :3, :12], cot[:, :3, :12]]), -1, -1)
    with jax.named_scope("prep"):
        prep = lax.cond(
            segment == 0,
            functools.partial(run_prep, False),
            functools.partial(run_prep, True),
            (x, cot, s1, s2, s3, adapters.reshape(768, 128)),
        )
        piece, prep = lax.optimization_barrier((piece, prep))
    with jax.named_scope("weights_neighbours"):
        p4 = neighbour_send(piece, 0, 1, 1)
        p6 = neighbour_send(piece, 1, 0, 0)
        p2 = neighbour_send(piece, -1, 0, 0)
        p7 = neighbour_send(piece, 0, 1, 0)
        p1 = neighbour_send(piece, 0, -1, 0)
        p5 = neighbour_send(piece, 0, 0, 1)
        p3 = neighbour_send(piece, 0, 0, -1)

    with jax.named_scope("bias"):
        table = jnp.where(segment == 1, table_deep, table_shallow)
        table = jnp.pad(table.T, ((0, 0), (0, 768 - table.shape[0])))
        index = jnp.pad(bias_index.T, ((0, 0), (0, 256 - WT)))
        bias, allowed = pl.pallas_call(
            bias_kernel,
            out_shape=(
                jax.ShapeDtypeStruct((HEADS, WT, 256), F32),
                jax.ShapeDtypeStruct((WT, 256), F32),
            ),
            in_specs=[SMEM, SMEM, VMEM, VMEM],
            out_specs=(VMEM, VMEM),
            name="bias_table",
        )(place, pole_mask, index, table)
    own, side, below, corner, grads = lax.cond(
        segment == 0,
        functools.partial(run_block, False),
        functools.partial(run_block, True),
        (place, piece, p1, p2, p3, p4, p5, p6, p7, bias, allowed, *prep),
    )

    with jax.named_scope("hand_over"):
        own, side = hand(own, 0, 0), hand(side, 0, 1)
        below, corner = hand(below, 1, 0), hand(corner, 1, 1)
    with jax.named_scope("adapter_sum"):
        grads = lax.all_to_all(grads.reshape(16, 48, 128), "lon", 0, 0)
        grads = lax.all_to_all(summed(grads), "lat", 0, 0)
        grads = lax.all_to_all(summed(grads), "lon", 0, 0)
        adapter_sum = grads.astype(F32).reshape(1, 98304)
    with jax.named_scope("assemble"):
        edge = jnp.where(segment == 0, 12, 6)
        column = lax.broadcasted_iota(jnp.int32, (1, 1, 24, 1), 2)
        main = jnp.concatenate([below, own], 1)
        strip = jnp.concatenate([corner, side], 1)
        strip = jnp.pad(strip, ((0, 0), (0, 0), (0, 12), (0, 0)))
        gradient = jnp.where(column < edge, strip, main)
    return gradient[None], adapter_sum


def solution(mesh):
    tokens = P("segment", None, "lat", "lon", None)
    in_specs = (
        tokens, tokens, P(), P(), P(), P(),
        P("lat", "lon"), P("lat", "lon"), P("lat", "lon"), P("lat", "lon"), P("segment", None),
    )
    return jax.shard_map(
        shards, mesh=mesh, in_specs=in_specs, out_specs=(tokens, P("segment", None)), check_vma=False
    )
```

```python
import functools

import jax
import jax.numpy as jnp
from jax import lax
from jax.experimental import pallas as pl
from jax.experimental.pallas import tpu as pltpu
from jax.sharding import PartitionSpec as P

WT = 144
HEADS = 8
HEAD = 64
QKV = 1536
INNER = 512
EPSILON = 1e-05
BF = jnp.bfloat16
F32 = jnp.float32
BOTH = ("lat", "lon")

PLACES = [(y, h, w, z) for y in range(8) for h in range(2) for w in range(2) for z in range(8)]
NUMBER = {place: i for i, place in enumerate(PLACES)}


def class_groups():
    groups = []
    for c in range(8):
        members = []
        for w in range(2):
            for z in range(8):
                for h in range(2):
                    members.append(NUMBER[((c - 4 * h - 2 * w - 3 * z) % 8, h, w, z)])
        groups.append(members)
    return groups


def neighbour_send(value, dx, dy, dz):
    route = []
    for y, h, w, z in PLACES:
        x = (2 * h + w + dx) % 4
        route.append((NUMBER[(y, h, w, z)], NUMBER[((y + dy) % 8, x // 2, x % 2, (z + dz) % 8)]))
    return lax.ppermute(value, BOTH, route)


def nt(a, b):
    return lax.dot_general(a, b, (((1,), (1,)), ((), ())), preferred_element_type=F32)


def nn(a, b):
    return lax.dot_general(a, b, (((1,), (0,)), ((), ())), preferred_element_type=F32)


def tn(a, b):
    return lax.dot_general(a, b, (((0,), (0,)), ((), ())), preferred_element_type=F32)


def pack_kernel(place_ref, qs_ref, ps_ref, qd_ref, pd_ref, out_ref):
    @pl.when(place_ref[2] == 0)
    def _():
        out_ref[0, 0:32, 0:96] = qs_ref[...]
        out_ref[0, 0:32, 96:128] = ps_ref[...].astype(F32).T.astype(BF)
        out_ref[0, 32:64, :] = jnp.zeros((32, 128), BF)

    @pl.when(place_ref[2] == 1)
    def _():
        out_ref[0, :, 0:96] = qd_ref[...]
        out_ref[0, :, 96:128] = pd_ref[...].astype(F32).T.astype(BF)

    own = out_ref[0]
    for i in range(1, 32):
        out_ref[i] = own


def window_row(shape, dim):
    token = lax.broadcasted_iota(jnp.int32, shape, dim)
    token = jnp.where(token >= 72, token - 72, token)
    row = jnp.zeros(shape, jnp.int32)
    for edge in range(12, 72, 12):
        row = row + (token >= edge).astype(jnp.int32)
    return row


def bias_kernel(place_ref, pole_ref, index_ref, table_ref, bias_ref, allowed_ref):
    for half in range(2):
        lanes = slice(128 * half, 128 * half + 128)
        index = index_ref[:, lanes]
        low = index & 127
        high = index >> 7
        for head in range(HEADS):
            found = jnp.zeros((WT, 128), F32)
            for chunk in range(6):
                entries = jnp.broadcast_to(
                    table_ref[head : head + 1, 128 * chunk : 128 * chunk + 128], (WT, 128)
                )
                taken = jnp.take_along_axis(entries, low, axis=1)
                found = taken if chunk == 0 else jnp.where(high == chunk, taken, found)
            bias_ref[head, :, lanes] = found
    first = place_ref[0] * 6 + 3
    key_row = window_row((WT, 256), 0)
    query_row = window_row((WT, 256), 1)
    key_ok = jnp.zeros((WT, 256), jnp.int32)
    key_region = jnp.zeros((WT, 256), jnp.int32)
    query_region = jnp.zeros((WT, 256), jnp.int32)
    for row in range(6):
        at = first + row
        moved = jnp.where(at >= 96, 1, 0)
        key_ok = jnp.where(key_row == row, pole_ref[at - 96 * moved], key_ok)
        key_region = jnp.where(key_row == row, moved, key_region)
        query_region = jnp.where(query_row == row, moved, query_region)
    good = (key_ok > 0) & (key_region == query_region)
    allowed_ref[...] = jnp.where(good, 1.0, 0.0)


def compact(wide):
    lane = lax.broadcasted_iota(jnp.int32, (wide.shape[0], 128), 1)
    chunks = []
    for group in range(4):
        a = [wide[:, 128 * (4 * group + i) : 128 * (4 * group + i) + 128] for i in range(4)]
        one = pltpu.roll(a[1], 96, 1)
        two = pltpu.roll(a[2], 64, 1)
        three = pltpu.roll(a[3], 32, 1)
        chunks.append(jnp.where(lane < 96, a[0], one))
        chunks.append(jnp.where(lane < 64, one, two))
        chunks.append(jnp.where(lane < 32, two, three))
    return chunks


def expand(chunks):
    lane = lax.broadcasted_iota(jnp.int32, chunks[0].shape, 1)
    wide = []
    for group in range(4):
        b = chunks[3 * group : 3 * group + 3]
        wide.append(jnp.where(lane < 96, b[0], 0.0))
        one = jnp.where(lane < 32, pltpu.roll(b[0], 32, 1), pltpu.roll(b[1], 32, 1))
        wide.append(jnp.where(lane < 96, one, 0.0))
        two = jnp.where(lane < 64, pltpu.roll(b[1], 64, 1), pltpu.roll(b[2], 64, 1))
        wide.append(jnp.where(lane < 96, two, 0.0))
        wide.append(jnp.where(lane < 96, pltpu.roll(b[2], 96, 1), 0.0))
    return [part.astype(BF) for part in wide]


def selector(shape, rank, k):
    row = lax.broadcasted_iota(jnp.int32, shape, 0)
    col = lax.broadcasted_iota(jnp.int32, shape, 1)
    if shape[0] == 32:
        hit = (row < rank) & (col == row + rank * k)
    else:
        hit = (col < rank) & (row == col + rank * k)
    return jnp.where(hit, 1.0, 0.0).astype(BF)


def sizes(deep):
    features, rank, windows = (1024, 24, 1) if deep else (512, 32, 2)
    counts = (features * rank // 128, rank * 12, 512 * rank // 128, rank * features // 128)
    starts = (0, counts[0], sum(counts[:2]), sum(counts[:3]))
    return features, rank, windows, counts, starts


def by_half(deep, ref):
    return jnp.concatenate([ref[0:WT], ref[WT : 2 * WT]], 1) if deep else ref[...]


def prep_kernel(
    deep,
    x_ref, c_ref, s1_ref, s2_ref, adapter_ref,
    normed_ref, cot_ref, scale_ref, low_q_ref, low_c_ref, aq_ref, bq_ref, ap_ref,
    xs, cols, aq_s, ap_s, bq_s, bp_s,
):
    features, rank, windows, counts, starts = sizes(deep)
    wide_row = 384 if deep else 128
    steps, per = wide_row // rank, wide_row // 128

    for i, dest in ((0, aq_s), (2, ap_s)):
        n = counts[i] // per
        parts = [adapter_ref[pl.ds(starts[i] + c, n, stride=per), :] for c in range(per)]
        packed = jnp.concatenate(parts, 1) if per > 1 else parts[0]
        packed = packed.astype(BF)
        for k in range(steps):
            dest[pl.ds(k, n, stride=steps), :] = nn(packed, selector((wide_row, 128), rank, k))
    if rank < 32:
        bq_s[...] = jnp.zeros_like(bq_s)
        bp_s[...] = jnp.zeros_like(bp_s)
    for c in range(12):
        bq_s[0:rank, 128 * c : 128 * c + 128] = adapter_ref[
            pl.ds(starts[1] + c, rank, stride=12), :
        ]
    for c in range(features // 128):
        bp_s[0:rank, 128 * c : 128 * c + 128] = adapter_ref[
            pl.ds(starts[3] + c, rank, stride=features // 128), :
        ]
    a_qkv = aq_s[0:features, 0:32].astype(BF)
    aq_ref[0:features] = a_qkv
    bq_ref[...] = bq_s[...].astype(BF)
    ap_ref[...] = ap_s[:, 0:32].astype(BF)
    b_proj = bp_s[:, 0:features].astype(BF)

    for source, which in ((c_ref, 1), (x_ref, 0)):
        for level in range(2):
            for row in range(6):
                if row < 3:
                    own = source[level, row + 3].astype(F32)
                else:
                    own = s1_ref[which, level, row - 3].astype(F32)
                side = s2_ref[which, level, row].astype(F32)
                at = 72 * level + 12 * row
                if deep:
                    for c in range(4):
                        lanes = slice(128 * c, 128 * c + 128)
                        cols[c, 0:12] = own[12:24, lanes]
                        cols[c, 12:24] = side[:, lanes]
                        for odd in range(2):
                            to = WT * odd + at
                            xs[to : to + 12, lanes] = cols[c, pl.ds(odd, 12, stride=2), :]
                else:
                    xs[at : at + 12, :] = own[6:18]
                    xs[at + 144 : at + 150, :] = own[18:24]
                    xs[at + 150 : at + 156, :] = side[0:6]
        if which == 1:
            cot_ref[...] = xs[...].astype(BF)
    x = by_half(deep, xs)
    centred = x - jnp.mean(x, axis=1, keepdims=True)
    scale = lax.rsqrt(jnp.mean(centred * centred, axis=1, keepdims=True) + EPSILON)
    normed = (centred * scale).astype(BF)
    if deep:
        normed_ref[0:WT] = normed[:, 0:512]
        normed_ref[WT : 2 * WT] = normed[:, 512:1024]
    else:
        normed_ref[...] = normed
    tokens = WT * windows
    scale_ref[0:tokens] = jnp.broadcast_to(scale, (tokens, 128))
    low_q_ref[0:tokens] = nn(normed, a_qkv).astype(BF)
    low_c_ref[0:tokens] = nt(by_half(deep, cot_ref), b_proj).astype(BF)


def block_kernel(
    deep,
    place_ref, p0, p1, p2, p3, p4, p5, p6, p7, bias_ref, allowed_ref,
    normed_ref, cot_ref, scale_ref, low_q_ref, low_c_ref, aq_ref, bq_ref, ap_ref,
    own_ref, side_ref, below_ref, corner_ref, grads_ref,
    weight, weight_p, xs, cols, aq_s, ap_s, flat,
):
    features, rank, windows, counts, starts = sizes(deep)
    wide_row = 384 if deep else 128
    steps, per = wide_row // rank, wide_row // 128
    tokens = WT * windows
    block = features // 16

    label = place_ref[1]
    for o, piece in enumerate((p0, p1, p2, p3, p4, p5, p6, p7)):
        for j in range(16):
            for h in range(2):
                y = lax.rem(label + o - 4 * h - 2 * (j // 8) - 3 * (j % 8) + 64, 8)
                at = pl.multiple_of((2 * y + h) * block, block)
                weight[pl.ds(at, block), 128 * j : 128 * j + 128] = piece[2 * j + h, :block]
    quarter = lax.broadcasted_iota(jnp.int32, (block, 128), 1) // 32
    for j in range(16):
        for m in range(4):
            tile = jnp.zeros((block, 128), F32)
            for k in range(4):
                at = (4 * m + k) * block
                part = weight[at : at + block, 128 * j : 128 * j + 128].astype(F32)
                if k < 3:
                    part = pltpu.roll(part, 32 * (k + 1), 1)
                tile = jnp.where(quarter == k, part, tile)
            weight_p[block * j : block * j + block, 128 * m : 128 * m + 128] = tile.astype(BF)

    normed = by_half(deep, normed_ref)
    cot_b = by_half(deep, cot_ref)
    low_q, low_c = low_q_ref[0:tokens], low_c_ref[0:tokens]
    a_qkv, b_qkv, a_proj = aq_ref[0:features], bq_ref[...], ap_ref[...]
    chunks = compact(nn(normed, weight[...]))
    low = nn(low_q, b_qkv)
    chunks = [chunks[c] + low[:, 128 * c : 128 * c + 128] for c in range(12)]
    d_mixed = nn(cot_b, weight_p[...]) + nt(low_c, a_proj)

    lane = lax.broadcasted_iota(jnp.int32, (WT, 128), 1)
    allowed = allowed_ref[:, :WT] > 0.0
    mixed = [[None] * windows for _ in range(4)]
    d_chunks = [[None] * windows for _ in range(12)]
    for w in range(windows):
        rows = slice(WT * w, WT * w + WT)
        for pair in range(4):
            q = chunks[pair][rows].astype(BF)
            k = chunks[4 + pair][rows].astype(BF)
            v = chunks[8 + pair][rows].astype(BF)
            d_o = d_mixed[rows, 128 * pair : 128 * pair + 128].astype(BF)
            found = []
            for half in range(2):
                mine = (lane >= 64) if half else (lane < 64)
                q_half = jnp.where(mine, q * 0.125, jnp.zeros_like(q))
                v_half = jnp.where(mine, v, jnp.zeros_like(v))
                s = nt(k, q_half) + bias_ref[2 * pair + half, :, :WT]
                s = jnp.where(allowed, s, -1000000000.0)
                e = jnp.exp(s - jnp.max(s, axis=0, keepdims=True))
                p = e / jnp.sum(e, axis=0, keepdims=True)
                p_b = p.astype(BF)
                d_p = nt(v_half, d_o)
                d_s = p * (d_p - jnp.sum(d_p * p, axis=0, keepdims=True))
                d_s = jnp.where(allowed, d_s, 0.0).astype(BF)
                found.append((tn(p_b, v), tn(d_s, k), nn(d_s, q), nn(p_b, d_o)))
            both = [jnp.where(lane < 64, one, two) for one, two in zip(*found)]
            mixed[pair][w] = both[0].astype(BF)
            d_chunks[pair][w] = both[1] * 0.125
            d_chunks[4 + pair][w] = both[2] * 0.125
            d_chunks[8 + pair][w] = both[3]

    def joined(parts, axis):
        return parts[0] if len(parts) == 1 else jnp.concatenate(parts, axis)

    mixed = joined([joined(parts, 0) for parts in mixed], 1)
    d_chunks = [joined(parts, 0) for parts in d_chunks]
    d_proj = joined([part.astype(BF) for part in d_chunks], 1)

    low_m = nn(mixed, a_proj).astype(BF)
    back = nt(d_proj, b_qkv).astype(BF)
    d_wide = joined(expand(d_chunks), 1)
    d_n = nt(d_wide, weight[...]) + nt(back, a_qkv)
    xhat = normed.astype(F32)
    mean_1 = jnp.mean(d_n, axis=1, keepdims=True)
    mean_2 = jnp.mean(d_n * xhat, axis=1, keepdims=True)
    scale = scale_ref[0:tokens, 0:1]
    xs[...] = cot_b.astype(F32) + scale * (d_n - mean_1 - xhat * mean_2)

    aq_s[:, 0:32] = tn(normed, back)
    ap_s[:, 0:32] = tn(mixed, low_c)
    d_bq = tn(low_q, d_proj)
    d_bp = tn(low_m, cot_b)
    for i, source in ((0, aq_s), (2, ap_s)):
        n = counts[i] // per
        total = jnp.zeros((n, wide_row), F32)
        for k in range(steps):
            part = source[pl.ds(k, n, stride=steps), :][:, 0:32].astype(BF)
            total = total + nn(part, selector((32, wide_row), rank, k))
        for c in range(per):
            flat[pl.ds(starts[i] + c, n, stride=per), :] = total[:, 128 * c : 128 * c + 128]
    for c in range(12):
        flat[pl.ds(starts[1] + c, rank, stride=12), :] = d_bq[0:rank, 128 * c : 128 * c + 128]
    for c in range(features // 128):
        flat[pl.ds(starts[3] + c, rank, stride=features // 128), :] = d_bp[
            0:rank, 128 * c : 128 * c + 128
        ]
    grads_ref[...] = flat[...].astype(BF)

    for level in range(2):
        for row in range(6):
            at = 72 * level + 12 * row
            main, strip = (own_ref, side_ref) if row < 3 else (below_ref, corner_ref)
            if deep:
                for c in range(4):
                    lanes = slice(128 * c, 128 * c + 128)
                    for odd in range(2):
                        to = 512 * odd + 128 * c
                        cols[c, pl.ds(odd, 12, stride=2), :] = xs[at : at + 12, to : to + 128]
                    main[level, row % 3, 12:24, lanes] = cols[c, 0:12].astype(BF)
                    strip[level, row % 3, :, lanes] = cols[c, 12:24].astype(BF)
            else:
                for c in range(4):
                    lanes = slice(128 * c, 128 * c + 128)
                    cols[c, 0:6] = xs[at + 150 : at + 156, lanes]
                    cols[c, 6:18] = xs[at : at + 12, lanes]
                    cols[c, 18:24] = xs[at + 144 : at + 150, lanes]
                    whole = cols[c].astype(BF)
                    main[level, row % 3, :, lanes] = whole
                    strip[level, row % 3, :, lanes] = whole[0:12]


VMEM = pl.BlockSpec(memory_space=pltpu.VMEM)
SMEM = pl.BlockSpec(memory_space=pltpu.SMEM)


def run_prep(deep, operands):
    features = 1024 if deep else 512
    shapes = (
        ((2 * WT, 512), BF), ((2 * WT, 512), BF), ((2 * WT, 128), F32), ((2 * WT, 32), BF),
        ((2 * WT, 32), BF), ((1024, 32), BF), ((32, QKV), BF), ((512, 32), BF),
    )
    return pl.pallas_call(
        functools.partial(prep_kernel, deep),
        out_shape=tuple(jax.ShapeDtypeStruct(*shape) for shape in shapes),
        in_specs=[VMEM] * len(operands),
        out_specs=(VMEM,) * len(shapes),
        scratch_shapes=[
            pltpu.VMEM((2 * WT, 512), F32),
            pltpu.VMEM((4, 24, 128), F32),
            pltpu.VMEM((features, 128), F32),
            pltpu.VMEM((512, 128), F32),
            pltpu.VMEM((32, QKV), F32),
            pltpu.VMEM((32, features), F32),
        ],
        compiler_params=pltpu.CompilerParams(vmem_limit_bytes=32 * 1024 * 1024),
        name="deep_prep" if deep else "shallow_prep",
    )(*operands)


def run_block(deep, operands):
    features = 1024 if deep else 512
    tokens = WT if deep else 2 * WT
    shapes = (
        ((2, 3, 24, 512), BF), ((2, 3, 12, 512), BF), ((2, 3, 24, 512), BF),
        ((2, 3, 12, 512), BF), ((768, 128), BF),
    )
    return pl.pallas_call(
        functools.partial(block_kernel, deep),
        out_shape=tuple(jax.ShapeDtypeStruct(*shape) for shape in shapes),
        in_specs=[SMEM] + [VMEM] * (len(operands) - 1),
        out_specs=(VMEM,) * 5,
        scratch_shapes=[
            pltpu.VMEM((features, 2048), BF),
            pltpu.VMEM((features, 512), BF),
            pltpu.VMEM((tokens, features), F32),
            pltpu.VMEM((4, 24, 128), F32),
            pltpu.VMEM((features, 128), F32),
            pltpu.VMEM((512, 128), F32),
            pltpu.VMEM((768, 128), F32),
        ],
        compiler_params=pltpu.CompilerParams(vmem_limit_bytes=56 * 1024 * 1024),
        name="deep_block" if deep else "shallow_block",
    )(*operands)


def sum_kernel(parts_ref, out_ref):
    total = parts_ref[0].astype(F32)
    for i in range(1, 16):
        total = total + parts_ref[i].astype(F32)
    out_ref[...] = jnp.broadcast_to(total.astype(BF)[None], out_ref.shape)


def summed(parts):
    return pl.pallas_call(
        sum_kernel,
        out_shape=jax.ShapeDtypeStruct((16, 48, 128), BF),
        in_specs=[pl.BlockSpec(memory_space=pltpu.VMEM)],
        out_specs=pl.BlockSpec(memory_space=pltpu.VMEM),
        name="sum_parts",
    )(parts)


def hand(value, d_lat, d_lon):
    route = []
    for s in range(2):
        for a in range(16):
            for b in range(16):
                to = (1 - s) * 256 + (a + d_lat) % 16 * 16 + (b + d_lon) % 16
                route.append((s * 256 + a * 16 + b, to))
    return lax.ppermute(value, ("segment", "lat", "lon"), route)


def shift(value, d_lat, d_lon):
    route = []
    for a in range(16):
        for b in range(16):
            route.append((a * 16 + b, (a + d_lat) % 16 * 16 + (b + d_lon) % 16))
    return lax.ppermute(value, BOTH, route)


def shards(
    saved_inputs, cotangent, pole_mask, bias_index, table_shallow, table_deep,
    qkv_shallow, proj_shallow, qkv_deep, proj_deep, adapters,
):
    segment = lax.axis_index("segment")
    lat = lax.axis_index("lat")
    lon = lax.axis_index("lon")
    x, cot = saved_inputs[0], cotangent[0]

    label = (4 * (lat % 2) + 2 * (lon // 8) + lat // 2 + 3 * (lon % 8)) % 8
    place = jnp.stack([lat, label, segment]).astype(jnp.int32)
    with jax.named_scope("pack"):
        own_w = pl.pallas_call(
            pack_kernel,
            out_shape=jax.ShapeDtypeStruct((32, 64, 128), BF),
            in_specs=[SMEM] + [VMEM] * 4,
            out_specs=VMEM,
            name="pack_weights",
        )(place, qkv_shallow, proj_shallow, qkv_deep, proj_deep)
    with jax.named_scope("weights_class"):
        piece = lax.all_to_all(own_w, BOTH, 0, 0, axis_index_groups=class_groups())
    with jax.named_scope("bias"):
        table = jnp.where(segment == 1, table_deep, table_shallow)
        table = jnp.pad(table.T, ((0, 0), (0, 768 - table.shape[0])))
        index = jnp.pad(bias_index.T, ((0, 0), (0, 256 - WT)))
        bias, allowed = pl.pallas_call(
            bias_kernel,
            out_shape=(
                jax.ShapeDtypeStruct((HEADS, WT, 256), F32),
                jax.ShapeDtypeStruct((WT, 256), F32),
            ),
            in_specs=[SMEM, SMEM, VMEM, VMEM],
            out_specs=(VMEM, VMEM),
            name="bias_table",
        )(place, pole_mask, index, table)
        piece, bias, allowed = lax.optimization_barrier((piece, bias, allowed))
    with jax.named_scope("halos"):
        s1 = shift(jnp.stack([x[:, :3], cot[:, :3]]), -1, 0)
        left = jnp.stack([x[:, 3:, :12], cot[:, 3:, :12]])
        s2 = shift(jnp.concatenate([left, s1[:, :, :, :12]], 2), 0, -1)
    with jax.named_scope("prep"):
        prep = lax.cond(
            segment == 0,
            functools.partial(run_prep, False),
            functools.partial(run_prep, True),
            (x, cot, s1, s2, adapters.reshape(768, 128)),
        )
    with jax.named_scope("weights_neighbours"):
        p4 = neighbour_send(piece, 0, 1, 1)
        p6 = neighbour_send(piece, 1, 0, 0)
        p2 = neighbour_send(piece, -1, 0, 0)
        p7 = neighbour_send(piece, 0, 1, 0)
        p1 = neighbour_send(piece, 0, -1, 0)
        p5 = neighbour_send(piece, 0, 0, 1)
        p3 = neighbour_send(piece, 0, 0, -1)

    own, side, below, corner, grads = lax.cond(
        segment == 0,
        functools.partial(run_block, False),
        functools.partial(run_block, True),
        (place, piece, p1, p2, p3, p4, p5, p6, p7, bias, allowed, *prep),
    )

    with jax.named_scope("hand_over"):
        own, side = hand(own, 0, 0), hand(side, 0, 1)
        below, corner = hand(below, 1, 0), hand(corner, 1, 1)
    with jax.named_scope("adapter_sum"):
        grads = lax.all_to_all(grads.reshape(16, 48, 128), "lon", 0, 0)
        grads = lax.all_to_all(summed(grads), "lat", 0, 0)
        grads = lax.all_to_all(summed(grads), "lon", 0, 0)
        adapter_sum = grads.astype(F32).reshape(1, 98304)
    with jax.named_scope("assemble"):
        edge = jnp.where(segment == 0, 12, 6)
        column = lax.broadcasted_iota(jnp.int32, (1, 1, 24, 1), 2)
        main = jnp.concatenate([below, own], 1)
        strip = jnp.concatenate([corner, side], 1)
        strip = jnp.pad(strip, ((0, 0), (0, 0), (0, 12), (0, 0)))
        gradient = jnp.where(column < edge, strip, main)
    return gradient[None], adapter_sum


def solution(mesh):
    tokens = P("segment", None, "lat", "lon", None)
    in_specs = (
        tokens, tokens, P(), P(), P(), P(),
        P("lat", "lon"), P("lat", "lon"), P("lat", "lon"), P("lat", "lon"), P("segment", None),
    )
    return jax.shard_map(
        shards, mesh=mesh, in_specs=in_specs, out_specs=(tokens, P("segment", None)), check_vma=False
    )
```

```python
import functools

import jax
import jax.numpy as jnp
from jax import lax
from jax.experimental import pallas as pl
from jax.experimental.pallas import tpu as pltpu
from jax.sharding import PartitionSpec as P

WT = 144
HEADS = 8
HEAD = 64
QKV = 1536
INNER = 512
EPSILON = 1e-05
BF = jnp.bfloat16
F32 = jnp.float32
BOTH = ("lat", "lon")

PLACES = [(y, h, w, z) for y in range(8) for h in range(2) for w in range(2) for z in range(8)]
NUMBER = {place: i for i, place in enumerate(PLACES)}


def class_groups():
    groups = []
    for c in range(8):
        members = []
        for w in range(2):
            for z in range(8):
                for h in range(2):
                    members.append(NUMBER[((c - 4 * h - 2 * w - 3 * z) % 8, h, w, z)])
        groups.append(members)
    return groups


def neighbour_send(value, dx, dy, dz):
    route = []
    for y, h, w, z in PLACES:
        x = (2 * h + w + dx) % 4
        route.append((NUMBER[(y, h, w, z)], NUMBER[((y + dy) % 8, x // 2, x % 2, (z + dz) % 8)]))
    return lax.ppermute(value, BOTH, route)


def nt(a, b):
    return lax.dot_general(a, b, (((1,), (1,)), ((), ())), preferred_element_type=F32)


def nn(a, b):
    return lax.dot_general(a, b, (((1,), (0,)), ((), ())), preferred_element_type=F32)


def tn(a, b):
    return lax.dot_general(a, b, (((0,), (0,)), ((), ())), preferred_element_type=F32)


def pack_kernel(place_ref, qs_ref, ps_ref, qd_ref, pd_ref, out_ref):
    @pl.when(place_ref[2] == 0)
    def _():
        out_ref[0, 0:32, 0:96] = qs_ref[...]
        out_ref[0, 0:32, 96:128] = ps_ref[...].astype(F32).T.astype(BF)
        out_ref[0, 32:64, :] = jnp.zeros((32, 128), BF)

    @pl.when(place_ref[2] == 1)
    def _():
        out_ref[0, :, 0:96] = qd_ref[...]
        out_ref[0, :, 96:128] = pd_ref[...].astype(F32).T.astype(BF)

    own = out_ref[0]
    for i in range(1, 32):
        out_ref[i] = own


def window_row(shape, dim):
    token = lax.broadcasted_iota(jnp.int32, shape, dim)
    token = jnp.where(token >= 144, token - 144, token)
    token = jnp.where(token >= 72, token - 72, token)
    row = jnp.zeros(shape, jnp.int32)
    for edge in range(12, 72, 12):
        row = row + (token >= edge).astype(jnp.int32)
    return row


def bias_kernel(place_ref, pole_ref, index_ref, table_ref, bias_ref, allowed_ref):
    lane = lax.broadcasted_iota(jnp.int32, (WT, 128), 1)
    for part in range(3):
        lanes = slice(128 * part, 128 * part + 128)
        index = index_ref[:, lanes]
        low = index & 127
        high = index >> 7

        def entries(head):
            found = None
            for chunk in range(6):
                row = table_ref[head : head + 1, 128 * chunk : 128 * chunk + 128]
                taken = jnp.take_along_axis(jnp.broadcast_to(row, (WT, 128)), low, axis=1)
                found = taken if chunk == 0 else jnp.where(high == chunk, taken, found)
            return found

        for pair in range(HEADS // 2):
            if part == 1:
                found = jnp.where(lane < WT - 128, entries(2 * pair), entries(2 * pair + 1))
            else:
                found = entries(2 * pair + part // 2)
            bias_ref[pair, :, lanes] = found
    first = place_ref[0] * 6 + 3
    key_row = window_row((WT, 384), 0)
    query_row = window_row((WT, 384), 1)
    key_ok = jnp.zeros((WT, 384), jnp.int32)
    key_region = jnp.zeros((WT, 384), jnp.int32)
    query_region = jnp.zeros((WT, 384), jnp.int32)
    for row in range(6):
        at = first + row
        moved = jnp.where(at >= 96, 1, 0)
        key_ok = jnp.where(key_row == row, pole_ref[at - 96 * moved], key_ok)
        key_region = jnp.where(key_row == row, moved, key_region)
        query_region = jnp.where(query_row == row, moved, query_region)
    good = (key_ok > 0) & (key_region == query_region)
    allowed_ref[...] = jnp.where(good, 1.0, 0.0)


def compact(wide):
    lane = lax.broadcasted_iota(jnp.int32, (wide.shape[0], 128), 1)
    chunks = []
    for group in range(4):
        a = [wide[:, 128 * (4 * group + i) : 128 * (4 * group + i) + 128] for i in range(4)]
        one = pltpu.roll(a[1], 96, 1)
        two = pltpu.roll(a[2], 64, 1)
        three = pltpu.roll(a[3], 32, 1)
        chunks.append(jnp.where(lane < 96, a[0], one))
        chunks.append(jnp.where(lane < 64, one, two))
        chunks.append(jnp.where(lane < 32, two, three))
    return chunks


def expand(chunks):
    lane = lax.broadcasted_iota(jnp.int32, chunks[0].shape, 1)
    wide = []
    for group in range(4):
        b = chunks[3 * group : 3 * group + 3]
        wide.append(jnp.where(lane < 96, b[0], 0.0))
        one = jnp.where(lane < 32, pltpu.roll(b[0], 32, 1), pltpu.roll(b[1], 32, 1))
        wide.append(jnp.where(lane < 96, one, 0.0))
        two = jnp.where(lane < 64, pltpu.roll(b[1], 64, 1), pltpu.roll(b[2], 64, 1))
        wide.append(jnp.where(lane < 96, two, 0.0))
        wide.append(jnp.where(lane < 96, pltpu.roll(b[2], 96, 1), 0.0))
    return [part.astype(BF) for part in wide]


def selector(shape, rank, k):
    row = lax.broadcasted_iota(jnp.int32, shape, 0)
    col = lax.broadcasted_iota(jnp.int32, shape, 1)
    if shape[0] == 32:
        hit = (row < rank) & (col == row + rank * k)
    else:
        hit = (col < rank) & (row == col + rank * k)
    return jnp.where(hit, 1.0, 0.0).astype(BF)


def sizes(deep):
    features, rank, windows = (1024, 24, 1) if deep else (512, 32, 2)
    counts = (features * rank // 128, rank * 12, 512 * rank // 128, rank * features // 128)
    starts = (0, counts[0], sum(counts[:2]), sum(counts[:3]))
    return features, rank, windows, counts, starts


def by_half(deep, ref):
    return jnp.concatenate([ref[0:WT], ref[WT : 2 * WT]], 1) if deep else ref[...]


def prep_kernel(
    deep,
    x_ref, c_ref, s1_ref, s2_ref, adapter_ref,
    normed_ref, cot_ref, scale_ref, low_q_ref, low_c_ref, aq_ref, bq_ref, ap_ref,
    xs, cols, aq_s, ap_s, bq_s, bp_s,
):
    features, rank, windows, counts, starts = sizes(deep)
    wide_row = 384 if deep else 128
    steps, per = wide_row // rank, wide_row // 128

    for i, dest in ((0, aq_s), (2, ap_s)):
        n = counts[i] // per
        parts = [adapter_ref[pl.ds(starts[i] + c, n, stride=per), :] for c in range(per)]
        packed = jnp.concatenate(parts, 1) if per > 1 else parts[0]
        packed = packed.astype(BF)
        for k in range(steps):
            dest[pl.ds(k, n, stride=steps), :] = nn(packed, selector((wide_row, 128), rank, k))
    if rank < 32:
        bq_s[...] = jnp.zeros_like(bq_s)
        bp_s[...] = jnp.zeros_like(bp_s)
    for c in range(12):
        bq_s[0:rank, 128 * c : 128 * c + 128] = adapter_ref[
            pl.ds(starts[1] + c, rank, stride=12), :
        ]
    for c in range(features // 128):
        bp_s[0:rank, 128 * c : 128 * c + 128] = adapter_ref[
            pl.ds(starts[3] + c, rank, stride=features // 128), :
        ]
    a_qkv = aq_s[0:features, 0:32].astype(BF)
    aq_ref[0:features] = a_qkv
    bq_ref[...] = bq_s[...].astype(BF)
    ap_ref[...] = ap_s[:, 0:32].astype(BF)
    b_proj = bp_s[:, 0:features].astype(BF)

    for source, which in ((c_ref, 1), (x_ref, 0)):
        for level in range(2):
            for row in range(6):
                if row < 3:
                    own = source[level, row + 3].astype(F32)
                else:
                    own = s1_ref[which, level, row - 3].astype(F32)
                side = s2_ref[which, level, row].astype(F32)
                at = 72 * level + 12 * row
                if deep:
                    for c in range(4):
                        lanes = slice(128 * c, 128 * c + 128)
                        cols[c, 0:12] = own[12:24, lanes]
                        cols[c, 12:24] = side[:, lanes]
                        for odd in range(2):
                            to = WT * odd + at
                            xs[to : to + 12, lanes] = cols[c, pl.ds(odd, 12, stride=2), :]
                else:
                    xs[at : at + 12, :] = own[6:18]
                    xs[at + 144 : at + 150, :] = own[18:24]
                    xs[at + 150 : at + 156, :] = side[0:6]
        if which == 1:
            cot_ref[...] = xs[...].astype(BF)
    x = by_half(deep, xs)
    centred = x - jnp.mean(x, axis=1, keepdims=True)
    scale = lax.rsqrt(jnp.mean(centred * centred, axis=1, keepdims=True) + EPSILON)
    normed = (centred * scale).astype(BF)
    if deep:
        normed_ref[0:WT] = normed[:, 0:512]
        normed_ref[WT : 2 * WT] = normed[:, 512:1024]
    else:
        normed_ref[...] = normed
    tokens = WT * windows
    scale_ref[0:tokens] = jnp.broadcast_to(scale, (tokens, 128))
    low_q_ref[0:tokens] = nn(normed, a_qkv).astype(BF)
    low_c_ref[0:tokens] = nt(by_half(deep, cot_ref), b_proj).astype(BF)


def block_kernel(
    deep,
    place_ref, p0, p1, p2, p3, p4, p5, p6, p7, bias_ref, allowed_ref,
    normed_ref, cot_ref, scale_ref, low_q_ref, low_c_ref, aq_ref, bq_ref, ap_ref,
    main_ref, strip_ref, grads_ref,
    weight, weight_p, xs, cols, aq_s, ap_s, flat,
):
    features, rank, windows, counts, starts = sizes(deep)
    wide_row = 384 if deep else 128
    steps, per = wide_row // rank, wide_row // 128
    tokens = WT * windows
    block = features // 16

    label = place_ref[1]
    for o, piece in enumerate((p0, p1, p2, p3, p4, p5, p6, p7)):
        for j in range(16):
            for h in range(2):
                y = lax.rem(label + o - 4 * h - 2 * (j // 8) - 3 * (j % 8) + 64, 8)
                at = pl.multiple_of((2 * y + h) * block, block)
                weight[pl.ds(at, block), 128 * j : 128 * j + 128] = piece[2 * j + h, :block]
    quarter = lax.broadcasted_iota(jnp.int32, (block, 128), 1) // 32
    for j in range(16):
        for m in range(4):
            tile = jnp.zeros((block, 128), F32)
            for k in range(4):
                at = (4 * m + k) * block
                part = weight[at : at + block, 128 * j : 128 * j + 128].astype(F32)
                if k < 3:
                    part = pltpu.roll(part, 32 * (k + 1), 1)
                tile = jnp.where(quarter == k, part, tile)
            weight_p[block * j : block * j + block, 128 * m : 128 * m + 128] = tile.astype(BF)

    normed = by_half(deep, normed_ref)
    cot_b = by_half(deep, cot_ref)
    low_q, low_c = low_q_ref[0:tokens], low_c_ref[0:tokens]
    a_qkv, b_qkv, a_proj = aq_ref[0:features], bq_ref[...], ap_ref[...]
    chunks = compact(nn(normed, weight[...]))
    low = nn(low_q, b_qkv)
    chunks = [chunks[c] + low[:, 128 * c : 128 * c + 128] for c in range(12)]
    d_mixed = nn(cot_b, weight_p[...]) + nt(low_c, a_proj)

    first_head = lax.broadcasted_iota(jnp.int32, (WT, 128), 1) < 64
    allowed = allowed_ref[:, : 2 * WT] > 0.0
    mixed = [[None] * windows for _ in range(4)]
    d_chunks = [[None] * windows for _ in range(12)]

    def by_head(value):
        zero = jnp.zeros_like(value)
        one, two = jnp.where(first_head, value, zero), jnp.where(first_head, zero, value)
        return jnp.concatenate([one, two], 0)

    def own_lanes(value):
        return jnp.where(first_head, value[0:WT], value[WT : 2 * WT])

    for w in range(windows):
        rows = slice(WT * w, WT * w + WT)
        for pair in range(4):
            q = by_head(chunks[pair][rows].astype(BF) * 0.125)
            k = chunks[4 + pair][rows].astype(BF)
            v = chunks[8 + pair][rows].astype(BF)
            d_o = by_head(d_mixed[rows, 128 * pair : 128 * pair + 128].astype(BF))
            s = nt(k, q) + bias_ref[pair, :, : 2 * WT]
            s = jnp.where(allowed, s, -1000000000.0)
            e = jnp.exp(s - jnp.max(s, axis=0, keepdims=True))
            p = e * (1.0 / jnp.sum(e, axis=0, keepdims=True))
            p_b = p.astype(BF)
            d_p = nt(v, d_o)
            d_s = p * (d_p - jnp.sum(d_p * p, axis=0, keepdims=True))
            d_s = jnp.where(allowed, d_s, 0.0).astype(BF)
            mixed[pair][w] = own_lanes(tn(p_b, v)).astype(BF)
            d_chunks[pair][w] = own_lanes(tn(d_s, k)) * 0.125
            d_chunks[4 + pair][w] = nn(d_s, q)
            d_chunks[8 + pair][w] = nn(p_b, d_o)

    def joined(parts, axis):
        return parts[0] if len(parts) == 1 else jnp.concatenate(parts, axis)

    mixed = joined([joined(parts, 0) for parts in mixed], 1)
    d_chunks = [joined(parts, 0) for parts in d_chunks]
    d_proj = joined([part.astype(BF) for part in d_chunks], 1)

    low_m = nn(mixed, a_proj).astype(BF)
    back = nt(d_proj, b_qkv).astype(BF)
    d_wide = joined(expand(d_chunks), 1)
    d_n = nt(d_wide, weight[...]) + nt(back, a_qkv)
    xhat = normed.astype(F32)
    mean_1 = jnp.mean(d_n, axis=1, keepdims=True)
    mean_2 = jnp.mean(d_n * xhat, axis=1, keepdims=True)
    scale = scale_ref[0:tokens, 0:1]
    xs[...] = cot_b.astype(F32) + scale * (d_n - mean_1 - xhat * mean_2)

    aq_s[:, 0:32] = tn(normed, back)
    ap_s[:, 0:32] = tn(mixed, low_c)
    d_bq = tn(low_q, d_proj)
    d_bp = tn(low_m, cot_b)
    for i, source in ((0, aq_s), (2, ap_s)):
        n = counts[i] // per
        total = jnp.zeros((n, wide_row), F32)
        for k in range(steps):
            part = source[pl.ds(k, n, stride=steps), :][:, 0:32].astype(BF)
            total = total + nn(part, selector((32, wide_row), rank, k))
        for c in range(per):
            flat[pl.ds(starts[i] + c, n, stride=per), :] = total[:, 128 * c : 128 * c + 128]
    for c in range(12):
        flat[pl.ds(starts[1] + c, rank, stride=12), :] = d_bq[0:rank, 128 * c : 128 * c + 128]
    for c in range(features // 128):
        flat[pl.ds(starts[3] + c, rank, stride=features // 128), :] = d_bp[
            0:rank, 128 * c : 128 * c + 128
        ]
    grads_ref[...] = flat[...].astype(BF)

    for level in range(2):
        for row in range(6):
            at = 72 * level + 12 * row
            if deep:
                for c in range(4):
                    lanes = slice(128 * c, 128 * c + 128)
                    for odd in range(2):
                        to = 512 * odd + 128 * c
                        cols[c, pl.ds(odd, 12, stride=2), :] = xs[at : at + 12, to : to + 128]
                    main_ref[level, row, 12:24, lanes] = cols[c, 0:12].astype(BF)
                    strip_ref[level, row, :, lanes] = cols[c, 12:24].astype(BF)
            else:
                for c in range(4):
                    lanes = slice(128 * c, 128 * c + 128)
                    cols[c, 0:6] = xs[at + 150 : at + 156, lanes]
                    cols[c, 6:18] = xs[at : at + 12, lanes]
                    cols[c, 18:24] = xs[at + 144 : at + 150, lanes]
                    whole = cols[c].astype(BF)
                    main_ref[level, row, :, lanes] = whole
                    strip_ref[level, row, :, lanes] = whole[0:12]


VMEM = pl.BlockSpec(memory_space=pltpu.VMEM)
SMEM = pl.BlockSpec(memory_space=pltpu.SMEM)


def run_prep(deep, operands):
    features = 1024 if deep else 512
    shapes = (
        ((2 * WT, 512), BF), ((2 * WT, 512), BF), ((2 * WT, 128), F32), ((2 * WT, 32), BF),
        ((2 * WT, 32), BF), ((1024, 32), BF), ((32, QKV), BF), ((512, 32), BF),
    )
    return pl.pallas_call(
        functools.partial(prep_kernel, deep),
        out_shape=tuple(jax.ShapeDtypeStruct(*shape) for shape in shapes),
        in_specs=[VMEM] * len(operands),
        out_specs=(VMEM,) * len(shapes),
        scratch_shapes=[
            pltpu.VMEM((2 * WT, 512), F32),
            pltpu.VMEM((4, 24, 128), F32),
            pltpu.VMEM((features, 128), F32),
            pltpu.VMEM((512, 128), F32),
            pltpu.VMEM((32, QKV), F32),
            pltpu.VMEM((32, features), F32),
        ],
        compiler_params=pltpu.CompilerParams(vmem_limit_bytes=32 * 1024 * 1024),
        name="deep_prep" if deep else "shallow_prep",
    )(*operands)


def run_block(deep, operands):
    features = 1024 if deep else 512
    tokens = WT if deep else 2 * WT
    shapes = (
        ((2, 6, 24, 512), BF), ((2, 6, 12, 512), BF), ((768, 128), BF),
    )
    return pl.pallas_call(
        functools.partial(block_kernel, deep),
        out_shape=tuple(jax.ShapeDtypeStruct(*shape) for shape in shapes),
        in_specs=[SMEM] + [VMEM] * (len(operands) - 1),
        out_specs=(VMEM,) * 3,
        scratch_shapes=[
            pltpu.VMEM((features, 2048), BF),
            pltpu.VMEM((features, 512), BF),
            pltpu.VMEM((tokens, features), F32),
            pltpu.VMEM((4, 24, 128), F32),
            pltpu.VMEM((features, 128), F32),
            pltpu.VMEM((512, 128), F32),
            pltpu.VMEM((768, 128), F32),
        ],
        compiler_params=pltpu.CompilerParams(vmem_limit_bytes=56 * 1024 * 1024),
        name="deep_block" if deep else "shallow_block",
    )(*operands)


def summed(parts):
    total = jnp.sum(parts.astype(F32), 0).astype(BF)
    return jnp.broadcast_to(total[None], (16, 48, 128))


def hand(value, d_lat, d_lon):
    route = []
    for s in range(2):
        for a in range(16):
            for b in range(16):
                to = (1 - s) * 256 + (a + d_lat) % 16 * 16 + (b + d_lon) % 16
                route.append((s * 256 + a * 16 + b, to))
    return lax.ppermute(value, ("segment", "lat", "lon"), route)


def shift(value, d_lat, d_lon):
    route = []
    for a in range(16):
        for b in range(16):
            route.append((a * 16 + b, (a + d_lat) % 16 * 16 + (b + d_lon) % 16))
    return lax.ppermute(value, BOTH, route)


def shards(
    saved_inputs, cotangent, pole_mask, bias_index, table_shallow, table_deep,
    qkv_shallow, proj_shallow, qkv_deep, proj_deep, adapters,
):
    segment = lax.axis_index("segment")
    lat = lax.axis_index("lat")
    lon = lax.axis_index("lon")
    x, cot = saved_inputs[0], cotangent[0]

    label = (4 * (lat % 2) + 2 * (lon // 8) + lat // 2 + 3 * (lon % 8)) % 8
    place = jnp.stack([lat, label, segment]).astype(jnp.int32)
    with jax.named_scope("pack"):
        own_w = pl.pallas_call(
            pack_kernel,
            out_shape=jax.ShapeDtypeStruct((32, 64, 128), BF),
            in_specs=[SMEM] + [VMEM] * 4,
            out_specs=VMEM,
            name="pack_weights",
        )(place, qkv_shallow, proj_shallow, qkv_deep, proj_deep)
    with jax.named_scope("weights_class"):
        piece = lax.all_to_all(own_w, BOTH, 0, 0, axis_index_groups=class_groups())
    with jax.named_scope("bias"):
        table = jnp.where(segment == 1, table_deep, table_shallow)
        table = jnp.pad(table.T, ((0, 0), (0, 768 - table.shape[0])))
        index = jnp.pad(jnp.concatenate([bias_index.T] * 2, 1), ((0, 0), (0, 384 - 2 * WT)))
        bias, allowed = pl.pallas_call(
            bias_kernel,
            out_shape=(
                jax.ShapeDtypeStruct((HEADS // 2, WT, 384), F32),
                jax.ShapeDtypeStruct((WT, 384), F32),
            ),
            in_specs=[SMEM, SMEM, VMEM, VMEM],
            out_specs=(VMEM, VMEM),
            name="bias_table",
        )(place, pole_mask, index, table)
        piece, bias, allowed = lax.optimization_barrier((piece, bias, allowed))
    with jax.named_scope("halos"):
        s1 = shift(jnp.stack([x[:, :3], cot[:, :3]]), -1, 0)
        left = jnp.stack([x[:, 3:, :12], cot[:, 3:, :12]])
        s2 = shift(jnp.concatenate([left, s1[:, :, :, :12]], 2), 0, -1)
    with jax.named_scope("prep"):
        prep = lax.cond(
            segment == 0,
            functools.partial(run_prep, False),
            functools.partial(run_prep, True),
            (x, cot, s1, s2, adapters.reshape(768, 128)),
        )
    with jax.named_scope("weights_neighbours"):
        p4 = neighbour_send(piece, 0, 1, 1)
        p6 = neighbour_send(piece, 1, 0, 0)
        p2 = neighbour_send(piece, -1, 0, 0)
        p7 = neighbour_send(piece, 0, 1, 0)
        p1 = neighbour_send(piece, 0, -1, 0)
        p5 = neighbour_send(piece, 0, 0, 1)
        p3 = neighbour_send(piece, 0, 0, -1)

    main, strip, grads = lax.cond(
        segment == 0,
        functools.partial(run_block, False),
        functools.partial(run_block, True),
        (place, piece, p1, p2, p3, p4, p5, p6, p7, bias, allowed, *prep),
    )

    with jax.named_scope("adapter_sum_lon"):
        grads = lax.all_to_all(grads.reshape(16, 48, 128), "lon", 0, 0)
    with jax.named_scope("hand_over"):
        strip = shift(strip, 0, 1)
        strip = jnp.pad(strip, ((0, 0), (0, 0), (0, 12), (0, 0)))
        column = lax.broadcasted_iota(jnp.int32, (1, 1, 24, 1), 2)
        main = jnp.where(column < jnp.where(segment == 0, 6, 12), strip, main)
        grads, main = lax.optimization_barrier((grads, main))
        own, below = hand(main[:, :3], 0, 0), hand(main[:, 3:], 1, 0)
    with jax.named_scope("adapter_sum_lat"):
        grads = lax.all_to_all(summed(grads), "lat", 0, 0)
        grads, own, below = lax.optimization_barrier((grads, own, below))
    with jax.named_scope("adapter_gather"):
        grads = lax.all_to_all(summed(grads), "lon", 0, 0)
        adapter_sum = grads.astype(F32).reshape(1, 98304)
    with jax.named_scope("assemble"):
        gradient = jnp.concatenate([below, own], 1)
    return gradient[None], adapter_sum


def solution(mesh):
    tokens = P("segment", None, "lat", "lon", None)
    in_specs = (
        tokens, tokens, P(), P(), P(), P(),
        P("lat", "lon"), P("lat", "lon"), P("lat", "lon"), P("lat", "lon"), P("segment", None),
    )
    return jax.shard_map(
        shards, mesh=mesh, in_specs=in_specs, out_specs=(tokens, P("segment", None)), check_vma=False
    )
```

```python
import functools

import jax
import jax.numpy as jnp
from jax import lax
from jax.experimental import pallas as pl
from jax.experimental.pallas import tpu as pltpu
from jax.sharding import PartitionSpec as P

WT = 144
HEADS = 8
HEAD = 64
QKV = 1536
INNER = 512
EPSILON = 1e-05
BF = jnp.bfloat16
F32 = jnp.float32
BOTH = ("lat", "lon")

PLACES = [(y, h, w, z) for y in range(8) for h in range(2) for w in range(2) for z in range(8)]
NUMBER = {place: i for i, place in enumerate(PLACES)}


def class_groups():
    groups = []
    for c in range(8):
        members = []
        for w in range(2):
            for z in range(8):
                for h in range(2):
                    members.append(NUMBER[((c - 4 * h - 2 * w - 3 * z) % 8, h, w, z)])
        groups.append(members)
    return groups


def neighbour_send(value, dx, dy, dz):
    route = []
    for y, h, w, z in PLACES:
        x = (2 * h + w + dx) % 4
        route.append((NUMBER[(y, h, w, z)], NUMBER[((y + dy) % 8, x // 2, x % 2, (z + dz) % 8)]))
    return lax.ppermute(value, BOTH, route)


def nt(a, b):
    return lax.dot_general(a, b, (((1,), (1,)), ((), ())), preferred_element_type=F32)


def nn(a, b):
    return lax.dot_general(a, b, (((1,), (0,)), ((), ())), preferred_element_type=F32)


def tn(a, b):
    return lax.dot_general(a, b, (((0,), (0,)), ((), ())), preferred_element_type=F32)


def pack_kernel(place_ref, qs_ref, ps_ref, qd_ref, pd_ref, out_ref):
    @pl.when(place_ref[2] == 0)
    def _():
        out_ref[0, 0:32, 0:96] = qs_ref[...]
        out_ref[0, 0:32, 96:128] = ps_ref[...].astype(F32).T.astype(BF)
        out_ref[0, 32:64, :] = jnp.zeros((32, 128), BF)

    @pl.when(place_ref[2] == 1)
    def _():
        out_ref[0, :, 0:96] = qd_ref[...]
        out_ref[0, :, 96:128] = pd_ref[...].astype(F32).T.astype(BF)

    own = out_ref[0]
    for i in range(1, 32):
        out_ref[i] = own


def window_row(shape, dim):
    token = lax.broadcasted_iota(jnp.int32, shape, dim)
    token = jnp.where(token >= 144, token - 144, token)
    token = jnp.where(token >= 72, token - 72, token)
    row = jnp.zeros(shape, jnp.int32)
    for edge in range(12, 72, 12):
        row = row + (token >= edge).astype(jnp.int32)
    return row


def bias_kernel(place_ref, pole_ref, index_ref, table_ref, bias_ref, allowed_ref):
    lane = lax.broadcasted_iota(jnp.int32, (WT, 128), 1)
    for part in range(3):
        lanes = slice(128 * part, 128 * part + 128)
        index = index_ref[:, lanes]
        low = index & 127
        high = index >> 7

        def entries(head):
            found = None
            for chunk in range(6):
                row = table_ref[head : head + 1, 128 * chunk : 128 * chunk + 128]
                taken = jnp.take_along_axis(jnp.broadcast_to(row, (WT, 128)), low, axis=1)
                found = taken if chunk == 0 else jnp.where(high == chunk, taken, found)
            return found

        for pair in range(HEADS // 2):
            if part == 1:
                found = jnp.where(lane < WT - 128, entries(2 * pair), entries(2 * pair + 1))
            else:
                found = entries(2 * pair + part // 2)
            bias_ref[pair, :, lanes] = found
    first = place_ref[0] * 6 + 3
    key_row = window_row((WT, 384), 0)
    query_row = window_row((WT, 384), 1)
    key_ok = jnp.zeros((WT, 384), jnp.int32)
    key_region = jnp.zeros((WT, 384), jnp.int32)
    query_region = jnp.zeros((WT, 384), jnp.int32)
    for row in range(6):
        at = first + row
        moved = jnp.where(at >= 96, 1, 0)
        key_ok = jnp.where(key_row == row, pole_ref[at - 96 * moved], key_ok)
        key_region = jnp.where(key_row == row, moved, key_region)
        query_region = jnp.where(query_row == row, moved, query_region)
    good = (key_ok > 0) & (key_region == query_region)
    allowed_ref[...] = jnp.where(good, 1.0, 0.0)


def compact(wide):
    lane = lax.broadcasted_iota(jnp.int32, (wide.shape[0], 128), 1)
    chunks = []
    for group in range(4):
        a = [wide[:, 128 * (4 * group + i) : 128 * (4 * group + i) + 128] for i in range(4)]
        one = pltpu.roll(a[1], 96, 1)
        two = pltpu.roll(a[2], 64, 1)
        three = pltpu.roll(a[3], 32, 1)
        chunks.append(jnp.where(lane < 96, a[0], one))
        chunks.append(jnp.where(lane < 64, one, two))
        chunks.append(jnp.where(lane < 32, two, three))
    return chunks


def expand(chunks):
    lane = lax.broadcasted_iota(jnp.int32, chunks[0].shape, 1)
    wide = []
    for group in range(4):
        b = chunks[3 * group : 3 * group + 3]
        wide.append(jnp.where(lane < 96, b[0], 0.0))
        one = jnp.where(lane < 32, pltpu.roll(b[0], 32, 1), pltpu.roll(b[1], 32, 1))
        wide.append(jnp.where(lane < 96, one, 0.0))
        two = jnp.where(lane < 64, pltpu.roll(b[1], 64, 1), pltpu.roll(b[2], 64, 1))
        wide.append(jnp.where(lane < 96, two, 0.0))
        wide.append(jnp.where(lane < 96, pltpu.roll(b[2], 96, 1), 0.0))
    return [part.astype(BF) for part in wide]


def selector(shape, rank, k):
    row = lax.broadcasted_iota(jnp.int32, shape, 0)
    col = lax.broadcasted_iota(jnp.int32, shape, 1)
    if shape[0] == 32:
        hit = (row < rank) & (col == row + rank * k)
    else:
        hit = (col < rank) & (row == col + rank * k)
    return jnp.where(hit, 1.0, 0.0).astype(BF)


def sizes(deep):
    features, rank, windows = (1024, 24, 1) if deep else (512, 32, 2)
    counts = (features * rank // 128, rank * 12, 512 * rank // 128, rank * features // 128)
    starts = (0, counts[0], sum(counts[:2]), sum(counts[:3]))
    return features, rank, windows, counts, starts


def by_half(deep, ref):
    return jnp.concatenate([ref[0:WT], ref[WT : 2 * WT]], 1) if deep else ref[...]


def prep_kernel(
    deep,
    x_ref, c_ref, s1_ref, s2_ref, adapter_ref,
    normed_ref, cot_ref, scale_ref, low_q_ref, low_c_ref, aq_ref, bq_ref, ap_ref,
    xs, cols, aq_s, ap_s, bq_s, bp_s,
):
    features, rank, windows, counts, starts = sizes(deep)
    wide_row = 384 if deep else 128
    steps, per = wide_row // rank, wide_row // 128

    for i, dest in ((0, aq_s), (2, ap_s)):
        n = counts[i] // per
        parts = [adapter_ref[pl.ds(starts[i] + c, n, stride=per), :] for c in range(per)]
        packed = jnp.concatenate(parts, 1) if per > 1 else parts[0]
        packed = packed.astype(BF)
        for k in range(steps):
            dest[pl.ds(k, n, stride=steps), :] = nn(packed, selector((wide_row, 128), rank, k))
    if rank < 32:
        bq_s[...] = jnp.zeros_like(bq_s)
        bp_s[...] = jnp.zeros_like(bp_s)
    for c in range(12):
        bq_s[0:rank, 128 * c : 128 * c + 128] = adapter_ref[
            pl.ds(starts[1] + c, rank, stride=12), :
        ]
    for c in range(features // 128):
        bp_s[0:rank, 128 * c : 128 * c + 128] = adapter_ref[
            pl.ds(starts[3] + c, rank, stride=features // 128), :
        ]
    a_qkv = aq_s[0:features, 0:32].astype(BF)
    aq_ref[0:features] = a_qkv
    bq_ref[...] = bq_s[...].astype(BF)
    ap_ref[...] = ap_s[:, 0:32].astype(BF)
    b_proj = bp_s[:, 0:features].astype(BF)

    for source, which in ((c_ref, 1), (x_ref, 0)):
        for level in range(2):
            for row in range(6):
                if row < 3:
                    own = source[level, row + 3].astype(F32)
                else:
                    own = s1_ref[which, level, row - 3].astype(F32)
                side = s2_ref[which, level, row].astype(F32)
                at = 72 * level + 12 * row
                if deep:
                    for c in range(4):
                        lanes = slice(128 * c, 128 * c + 128)
                        cols[c, 0:12] = own[12:24, lanes]
                        cols[c, 12:24] = side[:, lanes]
                        for odd in range(2):
                            to = WT * odd + at
                            xs[to : to + 12, lanes] = cols[c, pl.ds(odd, 12, stride=2), :]
                else:
                    xs[at : at + 12, :] = own[6:18]
                    xs[at + 144 : at + 150, :] = own[18:24]
                    xs[at + 150 : at + 156, :] = side[0:6]
        if which == 1:
            cot_ref[...] = xs[...].astype(BF)
    x = by_half(deep, xs)
    centred = x - jnp.mean(x, axis=1, keepdims=True)
    scale = lax.rsqrt(jnp.mean(centred * centred, axis=1, keepdims=True) + EPSILON)
    normed = (centred * scale).astype(BF)
    if deep:
        normed_ref[0:WT] = normed[:, 0:512]
        normed_ref[WT : 2 * WT] = normed[:, 512:1024]
    else:
        normed_ref[...] = normed
    tokens = WT * windows
    scale_ref[0:tokens] = jnp.broadcast_to(scale, (tokens, 128))
    low_q_ref[0:tokens] = nn(normed, a_qkv).astype(BF)
    low_c_ref[0:tokens] = nt(by_half(deep, cot_ref), b_proj).astype(BF)


def block_kernel(
    deep,
    place_ref, p0, p1, p2, p3, p4, p5, p6, p7, bias_ref, allowed_ref,
    normed_ref, cot_ref, scale_ref, low_q_ref, low_c_ref, aq_ref, bq_ref, ap_ref,
    main_ref, strip_ref, grads_ref,
    weight, weight_p, xs, cols, aq_s, ap_s, flat,
):
    features, rank, windows, counts, starts = sizes(deep)
    wide_row = 384 if deep else 128
    steps, per = wide_row // rank, wide_row // 128
    tokens = WT * windows
    block = features // 16

    label = place_ref[1]
    for o, piece in enumerate((p0, p1, p2, p3, p4, p5, p6, p7)):
        for j in range(16):
            for h in range(2):
                y = lax.rem(label + o - 4 * h - 2 * (j // 8) - 3 * (j % 8) + 64, 8)
                at = pl.multiple_of((2 * y + h) * block, block)
                weight[pl.ds(at, block), 128 * j : 128 * j + 128] = piece[2 * j + h, :block]
    quarter = lax.broadcasted_iota(jnp.int32, (block, 128), 1) // 32
    for j in range(16):
        for m in range(4):
            tile = jnp.zeros((block, 128), F32)
            for k in range(4):
                at = (4 * m + k) * block
                part = weight[at : at + block, 128 * j : 128 * j + 128].astype(F32)
                if k < 3:
                    part = pltpu.roll(part, 32 * (k + 1), 1)
                tile = jnp.where(quarter == k, part, tile)
            weight_p[block * j : block * j + block, 128 * m : 128 * m + 128] = tile.astype(BF)

    normed = by_half(deep, normed_ref)
    cot_b = by_half(deep, cot_ref)
    low_q, low_c = low_q_ref[0:tokens], low_c_ref[0:tokens]
    a_qkv, b_qkv, a_proj = aq_ref[0:features], bq_ref[...], ap_ref[...]
    chunks = compact(nn(normed, weight[...]))
    low = nn(low_q, b_qkv)
    chunks = [chunks[c] + low[:, 128 * c : 128 * c + 128] for c in range(12)]
    d_mixed = nn(cot_b, weight_p[...]) + nt(low_c, a_proj)

    first_head = lax.broadcasted_iota(jnp.int32, (WT, 128), 1) < 64
    allowed = allowed_ref[:, : 2 * WT] > 0.0
    mixed = [[None] * windows for _ in range(4)]
    d_chunks = [[None] * windows for _ in range(12)]

    def by_head(value):
        zero = jnp.zeros_like(value)
        one, two = jnp.where(first_head, value, zero), jnp.where(first_head, zero, value)
        return jnp.concatenate([one, two], 0)

    def own_lanes(value):
        return jnp.where(first_head, value[0:WT], value[WT : 2 * WT])

    for w in range(windows):
        rows = slice(WT * w, WT * w + WT)
        for pair in range(4):
            q = by_head(chunks[pair][rows].astype(BF) * 0.125)
            k = chunks[4 + pair][rows].astype(BF)
            v = chunks[8 + pair][rows].astype(BF)
            d_o = by_head(d_mixed[rows, 128 * pair : 128 * pair + 128].astype(BF))
            s = nt(k, q) + bias_ref[pair, :, : 2 * WT]
            s = jnp.where(allowed, s, -1000000000.0)
            e = jnp.exp(s - jnp.max(s, axis=0, keepdims=True))
            p = e * (1.0 / jnp.sum(e, axis=0, keepdims=True))
            p_b = p.astype(BF)
            d_p = nt(v, d_o)
            d_s = p * (d_p - jnp.sum(d_p * p, axis=0, keepdims=True))
            d_s = jnp.where(allowed, d_s, 0.0).astype(BF)
            mixed[pair][w] = own_lanes(tn(p_b, v)).astype(BF)
            d_chunks[pair][w] = own_lanes(tn(d_s, k)) * 0.125
            d_chunks[4 + pair][w] = nn(d_s, q)
            d_chunks[8 + pair][w] = nn(p_b, d_o)

    def joined(parts, axis):
        return parts[0] if len(parts) == 1 else jnp.concatenate(parts, axis)

    mixed = joined([joined(parts, 0) for parts in mixed], 1)
    d_chunks = [joined(parts, 0) for parts in d_chunks]
    d_proj = joined([part.astype(BF) for part in d_chunks], 1)

    low_m = nn(mixed, a_proj).astype(BF)
    back = nt(d_proj, b_qkv).astype(BF)
    d_wide = joined(expand(d_chunks), 1)
    d_n = nt(d_wide, weight[...]) + nt(back, a_qkv)
    xhat = normed.astype(F32)
    mean_1 = jnp.mean(d_n, axis=1, keepdims=True)
    mean_2 = jnp.mean(d_n * xhat, axis=1, keepdims=True)
    scale = scale_ref[0:tokens, 0:1]
    xs[...] = cot_b.astype(F32) + scale * (d_n - mean_1 - xhat * mean_2)

    aq_s[:, 0:32] = tn(normed, back)
    ap_s[:, 0:32] = tn(mixed, low_c)
    d_bq = tn(low_q, d_proj)
    d_bp = tn(low_m, cot_b)
    for i, source in ((0, aq_s), (2, ap_s)):
        n = counts[i] // per
        total = jnp.zeros((n, wide_row), F32)
        for k in range(steps):
            part = source[pl.ds(k, n, stride=steps), :][:, 0:32].astype(BF)
            total = total + nn(part, selector((32, wide_row), rank, k))
        for c in range(per):
            flat[pl.ds(starts[i] + c, n, stride=per), :] = total[:, 128 * c : 128 * c + 128]
    for c in range(12):
        flat[pl.ds(starts[1] + c, rank, stride=12), :] = d_bq[0:rank, 128 * c : 128 * c + 128]
    for c in range(features // 128):
        flat[pl.ds(starts[3] + c, rank, stride=features // 128), :] = d_bp[
            0:rank, 128 * c : 128 * c + 128
        ]
    grads_ref[...] = flat[...].astype(BF)

    for level in range(2):
        for row in range(6):
            at = 72 * level + 12 * row
            if deep:
                for c in range(4):
                    lanes = slice(128 * c, 128 * c + 128)
                    for odd in range(2):
                        to = 512 * odd + 128 * c
                        cols[c, pl.ds(odd, 12, stride=2), :] = xs[at : at + 12, to : to + 128]
                    main_ref[level, row, 12:24, lanes] = cols[c, 0:12].astype(BF)
                    strip_ref[level, row, :, lanes] = cols[c, 12:24].astype(BF)
            else:
                for c in range(4):
                    lanes = slice(128 * c, 128 * c + 128)
                    cols[c, 0:6] = xs[at + 150 : at + 156, lanes]
                    cols[c, 6:18] = xs[at : at + 12, lanes]
                    cols[c, 18:24] = xs[at + 144 : at + 150, lanes]
                    whole = cols[c].astype(BF)
                    main_ref[level, row, :, lanes] = whole
                    strip_ref[level, row, :, lanes] = whole[0:12]


VMEM = pl.BlockSpec(memory_space=pltpu.VMEM)
SMEM = pl.BlockSpec(memory_space=pltpu.SMEM)


def run_prep(deep, operands):
    features = 1024 if deep else 512
    shapes = (
        ((2 * WT, 512), BF), ((2 * WT, 512), BF), ((2 * WT, 128), F32), ((2 * WT, 32), BF),
        ((2 * WT, 32), BF), ((1024, 32), BF), ((32, QKV), BF), ((512, 32), BF),
    )
    return pl.pallas_call(
        functools.partial(prep_kernel, deep),
        out_shape=tuple(jax.ShapeDtypeStruct(*shape) for shape in shapes),
        in_specs=[VMEM] * len(operands),
        out_specs=(VMEM,) * len(shapes),
        scratch_shapes=[
            pltpu.VMEM((2 * WT, 512), F32),
            pltpu.VMEM((4, 24, 128), F32),
            pltpu.VMEM((features, 128), F32),
            pltpu.VMEM((512, 128), F32),
            pltpu.VMEM((32, QKV), F32),
            pltpu.VMEM((32, features), F32),
        ],
        compiler_params=pltpu.CompilerParams(vmem_limit_bytes=32 * 1024 * 1024),
        name="deep_prep" if deep else "shallow_prep",
    )(*operands)


def run_block(deep, operands):
    features = 1024 if deep else 512
    tokens = WT if deep else 2 * WT
    shapes = (
        ((2, 6, 24, 512), BF), ((2, 6, 12, 512), BF), ((768, 128), BF),
    )
    return pl.pallas_call(
        functools.partial(block_kernel, deep),
        out_shape=tuple(jax.ShapeDtypeStruct(*shape) for shape in shapes),
        in_specs=[SMEM] + [VMEM] * (len(operands) - 1),
        out_specs=(VMEM,) * 3,
        scratch_shapes=[
            pltpu.VMEM((features, 2048), BF),
            pltpu.VMEM((features, 512), BF),
            pltpu.VMEM((tokens, features), F32),
            pltpu.VMEM((4, 24, 128), F32),
            pltpu.VMEM((features, 128), F32),
            pltpu.VMEM((512, 128), F32),
            pltpu.VMEM((768, 128), F32),
        ],
        compiler_params=pltpu.CompilerParams(vmem_limit_bytes=56 * 1024 * 1024),
        name="deep_block" if deep else "shallow_block",
    )(*operands)


def summed(parts):
    total = jnp.sum(parts.astype(F32), 0).astype(BF)
    return jnp.broadcast_to(total[None], (16, 48, 128))


def hand(value, d_lat, d_lon):
    route = []
    for s in range(2):
        for a in range(16):
            for b in range(16):
                to = (1 - s) * 256 + (a + d_lat) % 16 * 16 + (b + d_lon) % 16
                route.append((s * 256 + a * 16 + b, to))
    return lax.ppermute(value, ("segment", "lat", "lon"), route)


def shift(value, d_lat, d_lon):
    route = []
    for a in range(16):
        for b in range(16):
            route.append((a * 16 + b, (a + d_lat) % 16 * 16 + (b + d_lon) % 16))
    return lax.ppermute(value, BOTH, route)


def shards(
    saved_inputs, cotangent, pole_mask, bias_index, table_shallow, table_deep,
    qkv_shallow, proj_shallow, qkv_deep, proj_deep, adapters,
):
    segment = lax.axis_index("segment")
    lat = lax.axis_index("lat")
    lon = lax.axis_index("lon")
    x, cot = saved_inputs[0], cotangent[0]

    label = (4 * (lat % 2) + 2 * (lon // 8) + lat // 2 + 3 * (lon % 8)) % 8
    place = jnp.stack([lat, label, segment]).astype(jnp.int32)
    with jax.named_scope("pack"):
        own_w = pl.pallas_call(
            pack_kernel,
            out_shape=jax.ShapeDtypeStruct((32, 64, 128), BF),
            in_specs=[SMEM] + [VMEM] * 4,
            out_specs=VMEM,
            name="pack_weights",
        )(place, qkv_shallow, proj_shallow, qkv_deep, proj_deep)
    with jax.named_scope("weights_class"):
        piece = lax.all_to_all(own_w, BOTH, 0, 0, axis_index_groups=class_groups())
    with jax.named_scope("bias"):
        table = jnp.where(segment == 1, table_deep, table_shallow)
        table = jnp.pad(table.T, ((0, 0), (0, 768 - table.shape[0])))
        index = jnp.pad(jnp.concatenate([bias_index.T] * 2, 1), ((0, 0), (0, 384 - 2 * WT)))
        bias, allowed = pl.pallas_call(
            bias_kernel,
            out_shape=(
                jax.ShapeDtypeStruct((HEADS // 2, WT, 384), F32),
                jax.ShapeDtypeStruct((WT, 384), F32),
            ),
            in_specs=[SMEM, SMEM, VMEM, VMEM],
            out_specs=(VMEM, VMEM),
            name="bias_table",
        )(place, pole_mask, index, table)
        piece, bias, allowed = lax.optimization_barrier((piece, bias, allowed))
    with jax.named_scope("halos"):
        s1 = shift(jnp.stack([x[:, :3], cot[:, :3]]), -1, 0)
        left = jnp.stack([x[:, 3:, :12], cot[:, 3:, :12]])
        s2 = shift(jnp.concatenate([left, s1[:, :, :, :12]], 2), 0, -1)
    with jax.named_scope("prep"):
        prep = lax.cond(
            segment == 0,
            functools.partial(run_prep, False),
            functools.partial(run_prep, True),
            (x, cot, s1, s2, adapters.reshape(768, 128)),
        )
    with jax.named_scope("weights_neighbours"):
        p4 = neighbour_send(piece, 0, 1, 1)
        p6 = neighbour_send(piece, 1, 0, 0)
        p2 = neighbour_send(piece, -1, 0, 0)
        p7 = neighbour_send(piece, 0, 1, 0)
        p1 = neighbour_send(piece, 0, -1, 0)
        p5 = neighbour_send(piece, 0, 0, 1)
        p3 = neighbour_send(piece, 0, 0, -1)

    main, strip, grads = lax.cond(
        segment == 0,
        functools.partial(run_block, False),
        functools.partial(run_block, True),
        (place, piece, p1, p2, p3, p4, p5, p6, p7, bias, allowed, *prep),
    )

    with jax.named_scope("adapter_sum_lon"):
        grads = lax.all_to_all(grads.reshape(16, 48, 128), "lon", 0, 0)
    with jax.named_scope("shift_back"):
        strip = shift(strip, 0, 1)
        strip = jnp.pad(strip, ((0, 0), (0, 0), (0, 12), (0, 0)))
        column = lax.broadcasted_iota(jnp.int32, (1, 1, 24, 1), 2)
        main = jnp.where(column < jnp.where(segment == 0, 6, 12), strip, main)
        below = shift(main[:, 3:], 1, 0)
    with jax.named_scope("adapter_sum_lat"):
        grads = lax.all_to_all(summed(grads), "lat", 0, 0)
        grads, below = lax.optimization_barrier((grads, below))
    with jax.named_scope("adapter_gather"):
        grads = lax.all_to_all(summed(grads), "lon", 0, 0)
        adapter_sum = grads.astype(F32).reshape(1, 98304)
    with jax.named_scope("hand_over"):
        gradient = hand(jnp.concatenate([below, main[:, :3]], 1), 0, 0)
    return gradient[None], adapter_sum


def solution(mesh):
    tokens = P("segment", None, "lat", "lon", None)
    in_specs = (
        tokens, tokens, P(), P(), P(), P(),
        P("lat", "lon"), P("lat", "lon"), P("lat", "lon"), P("lat", "lon"), P("segment", None),
    )
    return jax.shard_map(
        shards, mesh=mesh, in_specs=in_specs, out_specs=(tokens, P("segment", None)), check_vma=False
    )
```

```python
import functools

import jax
import jax.numpy as jnp
from jax import lax
from jax.experimental import pallas as pl
from jax.experimental.pallas import tpu as pltpu
from jax.sharding import PartitionSpec as P

WT = 144
HEADS = 8
HEAD = 64
QKV = 1536
INNER = 512
EPSILON = 1e-05
BF = jnp.bfloat16
F32 = jnp.float32
BOTH = ("lat", "lon")

PLACES = [(y, h, w, z) for y in range(8) for h in range(2) for w in range(2) for z in range(8)]
NUMBER = {place: i for i, place in enumerate(PLACES)}


def class_groups():
    groups = []
    for c in range(8):
        members = []
        for w in range(2):
            for z in range(8):
                for h in range(2):
                    members.append(NUMBER[((c - 4 * h - 2 * w - 3 * z) % 8, h, w, z)])
        groups.append(members)
    return groups


def neighbour_send(value, dx, dy, dz):
    route = []
    for y, h, w, z in PLACES:
        x = (2 * h + w + dx) % 4
        route.append((NUMBER[(y, h, w, z)], NUMBER[((y + dy) % 8, x // 2, x % 2, (z + dz) % 8)]))
    return lax.ppermute(value, BOTH, route)


def nt(a, b):
    return lax.dot_general(a, b, (((1,), (1,)), ((), ())), preferred_element_type=F32)


def nn(a, b):
    return lax.dot_general(a, b, (((1,), (0,)), ((), ())), preferred_element_type=F32)


def tn(a, b):
    return lax.dot_general(a, b, (((0,), (0,)), ((), ())), preferred_element_type=F32)


def pack_kernel(place_ref, qs_ref, ps_ref, qd_ref, pd_ref, out_ref):
    @pl.when(place_ref[2] == 0)
    def _():
        out_ref[0, 0:32, 0:96] = qs_ref[...]
        out_ref[0, 0:32, 96:128] = ps_ref[...].astype(F32).T.astype(BF)
        out_ref[0, 32:64, :] = jnp.zeros((32, 128), BF)

    @pl.when(place_ref[2] == 1)
    def _():
        out_ref[0, :, 0:96] = qd_ref[...]
        out_ref[0, :, 96:128] = pd_ref[...].astype(F32).T.astype(BF)

    own = out_ref[0]
    for i in range(1, 32):
        out_ref[i] = own


def window_row(shape, dim):
    token = lax.broadcasted_iota(jnp.int32, shape, dim)
    token = jnp.where(token >= 144, token - 144, token)
    token = jnp.where(token >= 72, token - 72, token)
    row = jnp.zeros(shape, jnp.int32)
    for edge in range(12, 72, 12):
        row = row + (token >= edge).astype(jnp.int32)
    return row


def bias_kernel(place_ref, pole_ref, index_ref, table_ref, bias_ref, allowed_ref):
    lane = lax.broadcasted_iota(jnp.int32, (WT, 128), 1)
    for part in range(3):
        lanes = slice(128 * part, 128 * part + 128)
        index = index_ref[:, lanes]
        low = index & 127
        high = index >> 7

        def entries(head):
            found = None
            for chunk in range(6):
                row = table_ref[head : head + 1, 128 * chunk : 128 * chunk + 128]
                taken = jnp.take_along_axis(jnp.broadcast_to(row, (WT, 128)), low, axis=1)
                found = taken if chunk == 0 else jnp.where(high == chunk, taken, found)
            return found

        for pair in range(HEADS // 2):
            if part == 1:
                found = jnp.where(lane < WT - 128, entries(2 * pair), entries(2 * pair + 1))
            else:
                found = entries(2 * pair + part // 2)
            bias_ref[pair, :, lanes] = found
    first = place_ref[0] * 6 + 3
    key_row = window_row((WT, 384), 0)
    query_row = window_row((WT, 384), 1)
    key_ok = jnp.zeros((WT, 384), jnp.int32)
    key_region = jnp.zeros((WT, 384), jnp.int32)
    query_region = jnp.zeros((WT, 384), jnp.int32)
    for row in range(6):
        at = first + row
        moved = jnp.where(at >= 96, 1, 0)
        key_ok = jnp.where(key_row == row, pole_ref[at - 96 * moved], key_ok)
        key_region = jnp.where(key_row == row, moved, key_region)
        query_region = jnp.where(query_row == row, moved, query_region)
    good = (key_ok > 0) & (key_region == query_region)
    allowed_ref[...] = jnp.where(good, 1.0, 0.0)


def compact(wide):
    lane = lax.broadcasted_iota(jnp.int32, (wide.shape[0], 128), 1)
    chunks = []
    for group in range(4):
        a = [wide[:, 128 * (4 * group + i) : 128 * (4 * group + i) + 128] for i in range(4)]
        one = pltpu.roll(a[1], 96, 1)
        two = pltpu.roll(a[2], 64, 1)
        three = pltpu.roll(a[3], 32, 1)
        chunks.append(jnp.where(lane < 96, a[0], one))
        chunks.append(jnp.where(lane < 64, one, two))
        chunks.append(jnp.where(lane < 32, two, three))
    return chunks


def expand(chunks):
    lane = lax.broadcasted_iota(jnp.int32, chunks[0].shape, 1)
    wide = []
    for group in range(4):
        b = chunks[3 * group : 3 * group + 3]
        wide.append(jnp.where(lane < 96, b[0], 0.0))
        one = jnp.where(lane < 32, pltpu.roll(b[0], 32, 1), pltpu.roll(b[1], 32, 1))
        wide.append(jnp.where(lane < 96, one, 0.0))
        two = jnp.where(lane < 64, pltpu.roll(b[1], 64, 1), pltpu.roll(b[2], 64, 1))
        wide.append(jnp.where(lane < 96, two, 0.0))
        wide.append(jnp.where(lane < 96, pltpu.roll(b[2], 96, 1), 0.0))
    return [part.astype(BF) for part in wide]


def selector(shape, rank, k):
    row = lax.broadcasted_iota(jnp.int32, shape, 0)
    col = lax.broadcasted_iota(jnp.int32, shape, 1)
    if shape[0] == 32:
        hit = (row < rank) & (col == row + rank * k)
    else:
        hit = (col < rank) & (row == col + rank * k)
    return jnp.where(hit, 1.0, 0.0).astype(BF)


def sizes(deep):
    features, rank, windows = (1024, 24, 1) if deep else (512, 32, 2)
    counts = (features * rank // 128, rank * 12, 512 * rank // 128, rank * features // 128)
    starts = (0, counts[0], sum(counts[:2]), sum(counts[:3]))
    return features, rank, windows, counts, starts


def by_half(deep, ref):
    return jnp.concatenate([ref[0:WT], ref[WT : 2 * WT]], 1) if deep else ref[...]


def prep_kernel(
    deep,
    x_ref, c_ref, s1_ref, s2_ref, adapter_ref,
    normed_ref, cot_ref, scale_ref, low_q_ref, low_c_ref, aq_ref, bq_ref, ap_ref,
    xs, cols, aq_s, ap_s, bq_s, bp_s,
):
    features, rank, windows, counts, starts = sizes(deep)
    wide_row = 384 if deep else 128
    steps, per = wide_row // rank, wide_row // 128

    for i, dest in ((0, aq_s), (2, ap_s)):
        n = counts[i] // per
        parts = [adapter_ref[pl.ds(starts[i] + c, n, stride=per), :] for c in range(per)]
        packed = jnp.concatenate(parts, 1) if per > 1 else parts[0]
        packed = packed.astype(BF)
        for k in range(steps):
            dest[pl.ds(k, n, stride=steps), :] = nn(packed, selector((wide_row, 128), rank, k))
    if rank < 32:
        bq_s[...] = jnp.zeros_like(bq_s)
        bp_s[...] = jnp.zeros_like(bp_s)
    for c in range(12):
        bq_s[0:rank, 128 * c : 128 * c + 128] = adapter_ref[
            pl.ds(starts[1] + c, rank, stride=12), :
        ]
    for c in range(features // 128):
        bp_s[0:rank, 128 * c : 128 * c + 128] = adapter_ref[
            pl.ds(starts[3] + c, rank, stride=features // 128), :
        ]
    a_qkv = aq_s[0:features, 0:32].astype(BF)
    aq_ref[0:features] = a_qkv
    bq_ref[...] = bq_s[...].astype(BF)
    ap_ref[...] = ap_s[:, 0:32].astype(BF)
    b_proj = bp_s[:, 0:features].astype(BF)

    for source, which in ((c_ref, 1), (x_ref, 0)):
        for level in range(2):
            for row in range(6):
                if row < 3:
                    own = source[level, row + 3].astype(F32)
                else:
                    own = s1_ref[which, level, row - 3].astype(F32)
                side = s2_ref[which, level, row].astype(F32)
                at = 72 * level + 12 * row
                if deep:
                    for c in range(4):
                        lanes = slice(128 * c, 128 * c + 128)
                        cols[c, 0:12] = own[12:24, lanes]
                        cols[c, 12:24] = side[:, lanes]
                        for odd in range(2):
                            to = WT * odd + at
                            xs[to : to + 12, lanes] = cols[c, pl.ds(odd, 12, stride=2), :]
                else:
                    xs[at : at + 12, :] = own[6:18]
                    xs[at + 144 : at + 150, :] = own[18:24]
                    xs[at + 150 : at + 156, :] = side[0:6]
        if which == 1:
            cot_ref[...] = xs[...].astype(BF)
    x = by_half(deep, xs)
    centred = x - jnp.mean(x, axis=1, keepdims=True)
    scale = lax.rsqrt(jnp.mean(centred * centred, axis=1, keepdims=True) + EPSILON)
    normed = (centred * scale).astype(BF)
    if deep:
        normed_ref[0:WT] = normed[:, 0:512]
        normed_ref[WT : 2 * WT] = normed[:, 512:1024]
    else:
        normed_ref[...] = normed
    tokens = WT * windows
    scale_ref[0:tokens] = jnp.broadcast_to(scale, (tokens, 128))
    low_q_ref[0:tokens] = nn(normed, a_qkv).astype(BF)
    low_c_ref[0:tokens] = nt(by_half(deep, cot_ref), b_proj).astype(BF)


def block_kernel(
    deep,
    place_ref, p0, p1, p2, p3, p4, p5, p6, p7, bias_ref, allowed_ref,
    normed_ref, cot_ref, scale_ref, low_q_ref, low_c_ref, aq_ref, bq_ref, ap_ref,
    main_ref, strip_ref, grads_ref,
    weight, weight_p, xs, cols, aq_s, ap_s, flat,
):
    features, rank, windows, counts, starts = sizes(deep)
    wide_row = 384 if deep else 128
    steps, per = wide_row // rank, wide_row // 128
    tokens = WT * windows
    block = features // 16

    label = place_ref[1]
    for o, piece in enumerate((p0, p1, p2, p3, p4, p5, p6, p7)):
        for j in range(16):
            for h in range(2):
                y = lax.rem(label + o - 4 * h - 2 * (j // 8) - 3 * (j % 8) + 64, 8)
                at = pl.multiple_of((2 * y + h) * block, block)
                weight[pl.ds(at, block), 128 * j : 128 * j + 128] = piece[2 * j + h, :block]
    quarter = lax.broadcasted_iota(jnp.int32, (block, 128), 1) // 32
    for j in range(16):
        for m in range(4):
            tile = jnp.zeros((block, 128), F32)
            for k in range(4):
                at = (4 * m + k) * block
                part = weight[at : at + block, 128 * j : 128 * j + 128].astype(F32)
                if k < 3:
                    part = pltpu.roll(part, 32 * (k + 1), 1)
                tile = jnp.where(quarter == k, part, tile)
            weight_p[block * j : block * j + block, 128 * m : 128 * m + 128] = tile.astype(BF)

    normed = by_half(deep, normed_ref)
    cot_b = by_half(deep, cot_ref)
    low_q, low_c = low_q_ref[0:tokens], low_c_ref[0:tokens]
    a_qkv, b_qkv, a_proj = aq_ref[0:features], bq_ref[...], ap_ref[...]
    chunks = compact(nn(normed, weight[...]))
    low = nn(low_q, b_qkv)
    chunks = [chunks[c] + low[:, 128 * c : 128 * c + 128] for c in range(12)]
    d_mixed = nn(cot_b, weight_p[...]) + nt(low_c, a_proj)

    first_head = lax.broadcasted_iota(jnp.int32, (WT, 128), 1) < 64
    allowed = allowed_ref[:, : 2 * WT] > 0.0
    mixed = [[None] * windows for _ in range(4)]
    d_chunks = [[None] * windows for _ in range(12)]

    def by_head(value):
        zero = jnp.zeros_like(value)
        one, two = jnp.where(first_head, value, zero), jnp.where(first_head, zero, value)
        return jnp.concatenate([one, two], 0)

    def own_lanes(value):
        return jnp.where(first_head, value[0:WT], value[WT : 2 * WT])

    for w in range(windows):
        rows = slice(WT * w, WT * w + WT)
        for pair in range(4):
            q = by_head(chunks[pair][rows].astype(BF) * 0.125)
            k = chunks[4 + pair][rows].astype(BF)
            v = chunks[8 + pair][rows].astype(BF)
            d_o = by_head(d_mixed[rows, 128 * pair : 128 * pair + 128].astype(BF))
            s = nt(k, q) + bias_ref[pair, :, : 2 * WT]
            s = jnp.where(allowed, s, -1000000000.0)
            e = jnp.exp(s - jnp.max(s, axis=0, keepdims=True))
            p = e * (1.0 / jnp.sum(e, axis=0, keepdims=True))
            p_b = p.astype(BF)
            d_p = nt(v, d_o)
            d_s = p * (d_p - jnp.sum(d_p * p, axis=0, keepdims=True))
            d_s = jnp.where(allowed, d_s, 0.0).astype(BF)
            mixed[pair][w] = own_lanes(tn(p_b, v)).astype(BF)
            d_chunks[pair][w] = own_lanes(tn(d_s, k)) * 0.125
            d_chunks[4 + pair][w] = nn(d_s, q)
            d_chunks[8 + pair][w] = nn(p_b, d_o)

    def joined(parts, axis):
        return parts[0] if len(parts) == 1 else jnp.concatenate(parts, axis)

    mixed = joined([joined(parts, 0) for parts in mixed], 1)
    d_chunks = [joined(parts, 0) for parts in d_chunks]
    d_proj = joined([part.astype(BF) for part in d_chunks], 1)

    low_m = nn(mixed, a_proj).astype(BF)
    back = nt(d_proj, b_qkv).astype(BF)
    d_wide = joined(expand(d_chunks), 1)
    d_n = nt(d_wide, weight[...]) + nt(back, a_qkv)
    xhat = normed.astype(F32)
    mean_1 = jnp.mean(d_n, axis=1, keepdims=True)
    mean_2 = jnp.mean(d_n * xhat, axis=1, keepdims=True)
    scale = scale_ref[0:tokens, 0:1]
    xs[...] = cot_b.astype(F32) + scale * (d_n - mean_1 - xhat * mean_2)

    aq_s[:, 0:32] = tn(normed, back)
    ap_s[:, 0:32] = tn(mixed, low_c)
    d_bq = tn(low_q, d_proj)
    d_bp = tn(low_m, cot_b)
    for i, source in ((0, aq_s), (2, ap_s)):
        n = counts[i] // per
        total = jnp.zeros((n, wide_row), F32)
        for k in range(steps):
            part = source[pl.ds(k, n, stride=steps), :][:, 0:32].astype(BF)
            total = total + nn(part, selector((32, wide_row), rank, k))
        for c in range(per):
            flat[pl.ds(starts[i] + c, n, stride=per), :] = total[:, 128 * c : 128 * c + 128]
    for c in range(12):
        flat[pl.ds(starts[1] + c, rank, stride=12), :] = d_bq[0:rank, 128 * c : 128 * c + 128]
    for c in range(features // 128):
        flat[pl.ds(starts[3] + c, rank, stride=features // 128), :] = d_bp[
            0:rank, 128 * c : 128 * c + 128
        ]
    grads_ref[...] = flat[...].astype(BF)

    for level in range(2):
        for row in range(6):
            at = 72 * level + 12 * row
            if deep:
                for c in range(4):
                    lanes = slice(128 * c, 128 * c + 128)
                    for odd in range(2):
                        to = 512 * odd + 128 * c
                        cols[c, pl.ds(odd, 12, stride=2), :] = xs[at : at + 12, to : to + 128]
                    main_ref[level, row, 12:24, lanes] = cols[c, 0:12].astype(BF)
                    strip_ref[level, row, :, lanes] = cols[c, 12:24].astype(BF)
            else:
                for c in range(4):
                    lanes = slice(128 * c, 128 * c + 128)
                    cols[c, 0:6] = xs[at + 150 : at + 156, lanes]
                    cols[c, 6:18] = xs[at : at + 12, lanes]
                    cols[c, 18:24] = xs[at + 144 : at + 150, lanes]
                    whole = cols[c].astype(BF)
                    main_ref[level, row, :, lanes] = whole
                    strip_ref[level, row, :, lanes] = whole[0:12]


VMEM = pl.BlockSpec(memory_space=pltpu.VMEM)
SMEM = pl.BlockSpec(memory_space=pltpu.SMEM)


def run_prep(deep, operands):
    features = 1024 if deep else 512
    shapes = (
        ((2 * WT, 512), BF), ((2 * WT, 512), BF), ((2 * WT, 128), F32), ((2 * WT, 32), BF),
        ((2 * WT, 32), BF), ((1024, 32), BF), ((32, QKV), BF), ((512, 32), BF),
    )
    return pl.pallas_call(
        functools.partial(prep_kernel, deep),
        out_shape=tuple(jax.ShapeDtypeStruct(*shape) for shape in shapes),
        in_specs=[VMEM] * len(operands),
        out_specs=(VMEM,) * len(shapes),
        scratch_shapes=[
            pltpu.VMEM((2 * WT, 512), F32),
            pltpu.VMEM((4, 24, 128), F32),
            pltpu.VMEM((features, 128), F32),
            pltpu.VMEM((512, 128), F32),
            pltpu.VMEM((32, QKV), F32),
            pltpu.VMEM((32, features), F32),
        ],
        compiler_params=pltpu.CompilerParams(vmem_limit_bytes=32 * 1024 * 1024),
        name="deep_prep" if deep else "shallow_prep",
    )(*operands)


def run_block(deep, operands):
    features = 1024 if deep else 512
    tokens = WT if deep else 2 * WT
    shapes = (
        ((2, 6, 24, 512), BF), ((2, 6, 12, 512), BF), ((768, 128), BF),
    )
    return pl.pallas_call(
        functools.partial(block_kernel, deep),
        out_shape=tuple(jax.ShapeDtypeStruct(*shape) for shape in shapes),
        in_specs=[SMEM] + [VMEM] * (len(operands) - 1),
        out_specs=(VMEM,) * 3,
        scratch_shapes=[
            pltpu.VMEM((features, 2048), BF),
            pltpu.VMEM((features, 512), BF),
            pltpu.VMEM((tokens, features), F32),
            pltpu.VMEM((4, 24, 128), F32),
            pltpu.VMEM((features, 128), F32),
            pltpu.VMEM((512, 128), F32),
            pltpu.VMEM((768, 128), F32),
        ],
        compiler_params=pltpu.CompilerParams(vmem_limit_bytes=56 * 1024 * 1024),
        name="deep_block" if deep else "shallow_block",
    )(*operands)


def summed(parts):
    total = jnp.sum(parts.astype(F32), 0).astype(BF)
    return jnp.broadcast_to(total[None], (16, 48, 128))


def hand(value, d_lat, d_lon):
    route = []
    for s in range(2):
        for a in range(16):
            for b in range(16):
                to = (1 - s) * 256 + (a + d_lat) % 16 * 16 + (b + d_lon) % 16
                route.append((s * 256 + a * 16 + b, to))
    return lax.ppermute(value, ("segment", "lat", "lon"), route)


def shift(value, d_lat, d_lon):
    route = []
    for a in range(16):
        for b in range(16):
            route.append((a * 16 + b, (a + d_lat) % 16 * 16 + (b + d_lon) % 16))
    return lax.ppermute(value, BOTH, route)


def shards(
    saved_inputs, cotangent, pole_mask, bias_index, table_shallow, table_deep,
    qkv_shallow, proj_shallow, qkv_deep, proj_deep, adapters,
):
    segment = lax.axis_index("segment")
    lat = lax.axis_index("lat")
    lon = lax.axis_index("lon")
    x, cot = saved_inputs[0], cotangent[0]

    label = (4 * (lat % 2) + 2 * (lon // 8) + lat // 2 + 3 * (lon % 8)) % 8
    place = jnp.stack([lat, label, segment]).astype(jnp.int32)
    with jax.named_scope("pack"):
        own_w = pl.pallas_call(
            pack_kernel,
            out_shape=jax.ShapeDtypeStruct((32, 64, 128), BF),
            in_specs=[SMEM] + [VMEM] * 4,
            out_specs=VMEM,
            name="pack_weights",
        )(place, qkv_shallow, proj_shallow, qkv_deep, proj_deep)
    with jax.named_scope("weights_class"):
        piece = lax.all_to_all(own_w, BOTH, 0, 0, axis_index_groups=class_groups())
    with jax.named_scope("bias"):
        table = jnp.where(segment == 1, table_deep, table_shallow)
        table = jnp.pad(table.T, ((0, 0), (0, 768 - table.shape[0])))
        index = jnp.pad(jnp.concatenate([bias_index.T] * 2, 1), ((0, 0), (0, 384 - 2 * WT)))
        bias, allowed = pl.pallas_call(
            bias_kernel,
            out_shape=(
                jax.ShapeDtypeStruct((HEADS // 2, WT, 384), F32),
                jax.ShapeDtypeStruct((WT, 384), F32),
            ),
            in_specs=[SMEM, SMEM, VMEM, VMEM],
            out_specs=(VMEM, VMEM),
            name="bias_table",
        )(place, pole_mask, index, table)
        piece, bias, allowed = lax.optimization_barrier((piece, bias, allowed))
    with jax.named_scope("halos"):
        s1 = shift(jnp.stack([x[:, :3], cot[:, :3]]), -1, 0)
        left = jnp.stack([x[:, 3:, :12], cot[:, 3:, :12]])
        s2 = shift(jnp.concatenate([left, s1[:, :, :, :12]], 2), 0, -1)
    with jax.named_scope("prep"):
        prep = lax.cond(
            segment == 0,
            functools.partial(run_prep, False),
            functools.partial(run_prep, True),
            (x, cot, s1, s2, adapters.reshape(768, 128)),
        )
    with jax.named_scope("weights_neighbours"):
        p4 = neighbour_send(piece, 0, 1, 1)
        p6 = neighbour_send(piece, 1, 0, 0)
        p2 = neighbour_send(piece, -1, 0, 0)
        p7 = neighbour_send(piece, 0, 1, 0)
        p1 = neighbour_send(piece, 0, -1, 0)
        p5 = neighbour_send(piece, 0, 0, 1)
        p3 = neighbour_send(piece, 0, 0, -1)

    main, strip, grads = lax.cond(
        segment == 0,
        functools.partial(run_block, False),
        functools.partial(run_block, True),
        (place, piece, p1, p2, p3, p4, p5, p6, p7, bias, allowed, *prep),
    )

    with jax.named_scope("adapter_sum_lon"):
        grads = lax.all_to_all(grads.reshape(16, 48, 128), "lon", 0, 0)
    with jax.named_scope("shift_back"):
        strip = shift(strip, 0, 1)
        strip = jnp.pad(strip, ((0, 0), (0, 0), (0, 12), (0, 0)))
        column = lax.broadcasted_iota(jnp.int32, (1, 1, 24, 1), 2)
        main = jnp.where(column < jnp.where(segment == 0, 6, 12), strip, main)
        below = shift(main[:, 3:], 1, 0)
    with jax.named_scope("adapter_sum_lat"):
        grads = lax.all_to_all(summed(grads), "lat", 0, 0)
    with jax.named_scope("adapter_gather"):
        grads = lax.all_to_all(summed(grads), "lon", 0, 0)
        adapter_sum = grads.astype(F32).reshape(1, 98304)
    with jax.named_scope("hand_over"):
        gradient = hand(jnp.concatenate([below, main[:, :3]], 1), 0, 0)
    return gradient[None], adapter_sum


def solution(mesh):
    tokens = P("segment", None, "lat", "lon", None)
    in_specs = (
        tokens, tokens, P(), P(), P(), P(),
        P("lat", "lon"), P("lat", "lon"), P("lat", "lon"), P("lat", "lon"), P("segment", None),
    )
    return jax.shard_map(
        shards, mesh=mesh, in_specs=in_specs, out_specs=(tokens, P("segment", None)), check_vma=False
    )
```
